256 devices in a mesh: section: 8 (over y, core), sp: 32 (over z, x).
Axes of the slice: x: 4, y: 4, z: 8, core: 2. Of those that a mesh axis runs over, the one named last changes fastest.
Arguments:
- section_input: bfloat16 [8, 384, 2, 12, 1536], P('section', 'sp'), may hold values from -6 to 6
- mirror_input: bfloat16 [8, 384, 2, 12, 1536], P('section', 'sp'), may hold values from -6 to 6
- saved_input: bfloat16 [8, 384, 2, 12, 1536], P('section', 'sp'), may hold values from -6 to 6
- output_grad: bfloat16 [8, 384, 2, 12, 1536], P('section', 'sp'), may hold values from -6 to 6
- qkv_weight: bfloat16 [8, 1536, 2304], P('section')
- out_weight: bfloat16 [8, 768, 1536], P('section', 'sp'), may hold values from -0.21875 to 0.21875
- norm_gain: float32 [8, 1536], P('section'), may hold values from 0.1 to 1.9
- land_bias: float32 [8, 1536], P('section'), may hold values from -3 to 3
- shift_offset: int32 [8], P('section'), may hold values from 1 to 5
- land_sea: int32 [384, 12], P('sp'), may hold values 0 or 1
- pole_pad: int32 [384, 12], replicated, may hold values from 0 to 1, as said below
Outputs:
- forward_out: bfloat16 [8, 384, 2, 12, 1536], P('section', 'sp')
- backward_out: bfloat16 [8, 384, 2, 12, 1536], P('section', 'sp')
- mirror_out: bfloat16 [8, 384, 2, 12, 1536], P('section', 'sp')
The draws below stay inside these ranges and needn't reach their ends.
Inputs may be any that keep to these rules, and one draw needn't show every extreme that they name: `pole_pad`: pole padding covers 1 to 4 rows at each end of every longitude column and nowhere else.
All inputs are finite; a program needn't handle non-finite values. No bound on the sum of `land_sea` on one device may be relied on, other than what follows from the above.
Results may differ from the reference program's by a relative error of at most 0.012.
Values may be sent and summed in bfloat16 or wider, within the bound.
No kernel may reach another device: no remote copies, remote signals or barrier semaphores. Data moves between devices by JAX's collectives and lax.ppermute only.
A program may use at most 128 MiB of HBM per device.

```python
import jax
import jax.numpy as jnp
from jax import lax

D = 1536
HEADS = 12
HEAD = 64
LATW = 12
LONW = 6
LEV = 2
LON = 12
SECTIONS = 8
NLAT = 384
N_SP = 32


def draw_qkv_weight(key, part):
    key = jax.random.fold_in(key, 11)
    width = HEADS * HEAD
    shape = (SECTIONS, D, 3 * width)
    base = jax.random.normal(key, shape, jnp.float32) * D ** (-0.5)
    return base.astype(jnp.bfloat16)


def draw_pole_pad(key, part):
    key = jax.random.fold_in(key, 5)
    north_key, south_key = jax.random.split(key)
    north_rows = jax.random.randint(north_key, (LON,), 1, 5)
    south_rows = jax.random.randint(south_key, (LON,), 1, 5)
    latitude = jnp.arange(NLAT)[:, None]
    inside = (latitude >= north_rows[None, :]) & (latitude < NLAT - south_rows[None, :])
    return inside.astype(jnp.int32)


def touch_ends(entries, own_key, smallest, high):
    extent = entries.shape
    spot = [jax.random.randint(jax.random.fold_in(own_key, axis), (), 0, extent[axis]) for axis in range(len(extent))]
    entries = entries.at[tuple(spot)].set(smallest)
    longest = extent.index(max(extent))
    spot[longest] = (spot[longest] + 1) % extent[longest]
    return entries.at[tuple(spot)].set(high)


def block_levels(own_key, shape, cuts, least, high):
    loudness, own = 1.0, jax.random.fold_in(own_key, 6)
    for position, parts in cuts:
        heights = jnp.exp(jax.random.uniform(jax.random.fold_in(own, position), (parts,), jnp.float32, least / len(cuts), high / len(cuts)))
        loudness = loudness * jnp.repeat(heights, shape[position] // parts).reshape([-1 if axis == position else 1 for axis in range(len(shape))])
    return loudness


def normal_values(key, extent, scale, bound, cuts=(), kind=jnp.bfloat16):
    entries = scale * jax.random.normal(key, extent, jnp.float32)
    if cuts:
        entries = entries * block_levels(key, extent, cuts, -0.22, 0.18)
    return jnp.clip(entries, -bound, bound).astype(kind)


def setup_inputs(seed: int = 0) -> dict:
    key_of = jax.random.split(jax.random.key(seed), 12)
    section_input = normal_values(key_of[0], (SECTIONS, NLAT, LEV, LON, D), 1.0, 6.0, ((0, 8), (1, 32)))
    mirror_input = normal_values(key_of[1], (SECTIONS, NLAT, LEV, LON, D), 1.0, 6.0, ((0, 8), (1, 32)))
    saved_input = normal_values(key_of[2], (SECTIONS, NLAT, LEV, LON, D), 1.0, 6.0, ((0, 8), (1, 32)))
    output_grad = normal_values(key_of[3], (SECTIONS, NLAT, LEV, LON, D), 1.0, 6.0, ((0, 8), (1, 32)))
    qkv_weight = draw_qkv_weight(jax.random.fold_in(key_of[11], 71), 0)
    out_weight = normal_values(key_of[5], (SECTIONS, HEADS * HEAD, D), (HEADS * HEAD) ** -0.5, 0.21875, ((0, 8), (1, 32)))
    norm_gain = jnp.clip(1.0 + 0.18 * jax.random.normal(key_of[6], (SECTIONS, D), jnp.float32), 0.1, 1.9)
    land_bias = normal_values(key_of[7], (SECTIONS, D), 0.5, 3.0, ((0, 8),), jnp.float32)
    shift_offset = touch_ends(jax.random.randint(key_of[8], (SECTIONS,), 1, LONW), jax.random.fold_in(key_of[8], 1), 1, LONW - 1).astype(jnp.int32)
    land_sea = touch_ends((jax.random.randint(key_of[9], (NLAT, LON), 0, 3) < 1).astype(jnp.int32), jax.random.fold_in(key_of[9], 1), 0, 1)
    pole_pad = draw_pole_pad(jax.random.fold_in(key_of[11], 71), 0)
    return {"section_input": section_input, "mirror_input": mirror_input, "saved_input": saved_input, "output_grad": output_grad, "qkv_weight": qkv_weight, "out_weight": out_weight, "norm_gain": norm_gain, "land_bias": land_bias, "shift_offset": shift_offset, "land_sea": land_sea, "pole_pad": pole_pad}


def normed_rows(inputs, norm_scale, land_shift, land_cells):
    average = lax.optimization_barrier(jnp.mean(inputs, axis=-1, keepdims=True))
    centered = inputs - average
    spread = lax.optimization_barrier(jnp.mean(centered * centered, axis=-1, keepdims=True))
    scaled = centered * lax.rsqrt(spread + 1e-05) * norm_scale
    land_term = land_cells[:, None, :, None].astype(inputs.dtype) * land_shift
    return (scaled + land_term).astype(jnp.bfloat16)

def project(normed, weight):
    return jnp.dot(normed, weight, preferred_element_type=jnp.float32).astype(jnp.bfloat16)

def window_attention(packed, key_valid, pole_split, offset):
    total_rows, levels, longitudes, width = packed.shape
    row_windows = total_rows // LATW
    col_windows = longitudes // LONW
    per_window = LATW * levels * LONW
    rolled = jnp.roll(packed, -offset, axis=2)
    rolled_valid = jnp.roll(key_valid, -offset, axis=1)
    pieces = rolled.reshape(row_windows, LATW, levels, col_windows, LONW, 3, HEADS, HEAD)
    pieces = pieces.transpose(5, 0, 3, 6, 1, 2, 4, 7).reshape(3, row_windows, col_windows, HEADS, per_window, HEAD)
    queries = pieces[0].astype(jnp.float32)
    key_vecs = pieces[1].astype(jnp.float32)
    value_vecs = pieces[2].astype(jnp.float32)
    key_ok = rolled_valid.reshape(row_windows, LATW, col_windows, LONW).transpose(0, 2, 1, 3)
    key_ok = jnp.broadcast_to(key_ok[:, :, :, None, :], (row_windows, col_windows, LATW, levels, LONW))
    key_ok = key_ok.reshape(row_windows, col_windows, per_window)
    upper = jnp.arange(per_window) // (levels * LONW) >= LATW // 2
    same_half = upper[:, None] == upper[None, :]
    region_ok = same_half[None] | jnp.logical_not(pole_split)[:, None, None]
    diagonal = jnp.eye(per_window, dtype=bool)
    allowed = key_ok[:, :, None, :] & region_ok[:, None] | diagonal
    scores = jnp.einsum('cwhqd,cwhkd->cwhqk', queries, key_vecs) * HEAD ** (-0.5)
    scores = jnp.where(allowed[:, :, None], scores, -1000000000.0)
    largest = lax.optimization_barrier(jnp.max(scores, axis=-1, keepdims=True))
    expo = jnp.exp(scores - largest)
    probs = (expo / lax.optimization_barrier(jnp.sum(expo, axis=-1, keepdims=True))).astype(jnp.bfloat16)
    mixed = jnp.einsum('cwhqk,cwhkd->cwhqd', probs.astype(jnp.float32), value_vecs).astype(jnp.bfloat16)
    mixed = mixed.reshape(row_windows, col_windows, HEADS, LATW, levels, LONW, HEAD)
    mixed = mixed.transpose(0, 3, 4, 1, 5, 2, 6).reshape(total_rows, levels, longitudes, HEADS * HEAD)
    return jnp.roll(mixed, offset, axis=2)

def reference(section_input, mirror_input, saved_input, output_grad, qkv_weight, out_weight, norm_gain, land_bias, shift_offset, land_sea, pole_pad):
    half_rows = LATW // 2
    key_valid = jnp.roll(pole_pad, half_rows, axis=0) > 0
    pole_split = jnp.arange(N_SP) == 0

    def block(inputs, section_number):
        normed = normed_rows(inputs, norm_gain[section_number], land_bias[section_number], land_sea)
        packed = project(normed, qkv_weight[section_number])
        mixed = window_attention(jnp.roll(packed, half_rows, axis=0), key_valid, pole_split, shift_offset[section_number])
        mixed = jnp.roll(mixed, -half_rows, axis=0)
        summed = inputs + jnp.dot(mixed, out_weight[section_number], preferred_element_type=jnp.float32)
        return summed.astype(jnp.bfloat16)
    outputs = []
    gradients = []
    for section_number in range(SECTIONS):
        decoder = section_number >= SECTIONS // 2
        start = section_input[section_number].astype(jnp.float32)
        if decoder:
            start = start + mirror_input[section_number].astype(jnp.float32)
        outputs.append(block(start, section_number))
        upstream = output_grad[section_number].astype(jnp.float32)
        if not decoder:
            upstream = upstream + mirror_input[section_number].astype(jnp.float32)
        cotangent = upstream.astype(jnp.bfloat16)
        saved = saved_input[section_number].astype(jnp.float32)
        _, pullback = jax.vjp(lambda inputs: block(inputs, section_number), saved)
        gradients.append(pullback(cotangent)[0].astype(jnp.bfloat16))
    output_all = jnp.stack(outputs)
    grad_all = jnp.stack(gradients)
    forward_out = jnp.roll(output_all, 1, axis=0)
    backward_out = jnp.roll(grad_all, -1, axis=0)
    payload = jnp.concatenate([output_all[:SECTIONS // 2], grad_all[SECTIONS // 2:]], axis=0)
    mirror_out = payload[::-1]
    return (forward_out, backward_out, mirror_out)
```

```python
import functools

import jax
import jax.numpy as jnp
import numpy as np
from jax import lax
from jax.experimental import pallas as pl
from jax.experimental.pallas import tpu as pltpu
from jax.sharding import PartitionSpec as P

HEADS = 12
HEAD = 64
LATW = 12
LONW = 6
LEV = 2
LON = 12
HALF = LATW // 2 * LEV * LON
PART = HALF // 2
PAD = 80
WIN = 2 * PAD
PAIR = 2 * HEAD
PAIRS = HEADS // 2
GROUP = 2 * PAIR
X_SIZE = 4
BLOCKS = 9
LOADS = 12
GROUPS = HEADS * HEAD // GROUP
BF = jnp.bfloat16
F32 = jnp.float32
VMEM = 60 * 2**20


def row_parts():
    rows = np.arange(WIN)
    side, within = rows // PAD, rows % PAD
    spot = side * LONW + within % (LONW * LEV) // LEV
    return within < PART, within // (LONW * LEV), spot, within % LEV


def place_table():
    real, lat, spot, level = (part[:, None] for part in row_parts())
    token = np.arange(HALF)[None, :]
    same = real & (lat == token // (LON * LEV)) & (level == token % LEV)
    return np.where(same, (token // LEV % LON - spot) % LON, -1).astype(np.int32)


def cell_table():
    real, lat, spot, _ = (part[:, None] for part in row_parts())
    shifts = np.where(real, (np.arange(LON)[None, :] - spot) % LON, -1)
    return np.concatenate([shifts, lat], axis=1).astype(np.int32)


def land_table():
    token = np.arange(HALF)[:, None]
    return np.concatenate([token // (LON * LEV), token // LEV % LON], axis=1).astype(np.int32)


def dot(a, b):
    return jnp.dot(a, b, preferred_element_type=F32)


def dot_nt(a, b):
    return lax.dot_general(a, b, (((1,), (1,)), ((), ())), preferred_element_type=F32)


def dot_tn(a, b):
    return lax.dot_general(a, b, (((0,), (0,)), ((), ())), preferred_element_type=F32)


def one_hot(table_ref, offset):
    return (table_ref[...] == offset).astype(F32).astype(BF)


def is_decoder():
    return (lax.axis_index("section") >= lax.axis_size("section") // 2).astype(F32)


def tokens(ref):
    return ref[...].reshape(-1, ref.shape[-1])


def norm_parts(rows):
    centered = rows - jnp.mean(rows, axis=-1, keepdims=True)
    spread = jnp.mean(centered * centered, axis=-1, keepdims=True)
    return centered, lax.rsqrt(spread + 1e-05)


def prepare_kernel(num, sec, mir, sav, grd, gain, bias, land, table, where, local, down, up):
    half = pl.program_id(0)
    decoder = is_decoder()
    place = one_hot(table, num[0])
    lat, lon = where[:, 0:1], where[:, 1:2]
    cells = land[...].astype(F32)
    line = jnp.zeros((HALF, LON), F32)
    for row in range(LATW // 2):
        both = jnp.where(half == 0, cells[row : row + 1], cells[row + LATW // 2 : row + LATW // 2 + 1])
        line = jnp.where(lat == row, both, line)
    spots = lax.broadcasted_iota(jnp.int32, (HALF, LON), 1) == lon
    on_land = jnp.sum(jnp.where(spots, line, 0.0), axis=-1, keepdims=True)
    land_term = on_land * bias[...]
    mirror = tokens(mir).astype(F32)
    start = tokens(sec).astype(F32) + decoder * mirror
    cot = (tokens(grd).astype(F32) + (1.0 - decoder) * mirror).astype(BF)

    def normed(rows):
        centered, scale = norm_parts(rows)
        return (centered * scale * gain[...] + land_term).astype(BF)

    for i, rows in enumerate((normed(start), normed(tokens(sav).astype(F32)), cot)):
        placed = dot(place, rows).astype(BF)

        @pl.when(half == 0)
        def _():
            local[i] = placed[:PAD]
            up[i] = placed[PAD:]

        @pl.when(half == 1)
        def _():
            local[i] = placed[PAD:]
            down[i] = placed[:PAD]


def valid_cells(pad, cells, offset, first_row):
    lat = cells[:, LON : LON + 1]
    line = jnp.zeros((WIN, LON), F32)
    for row in range(LATW // 2):
        line = jnp.where(lat == row, pad[pl.ds(first_row + row, 1), :].astype(F32), line)
    return jnp.max(jnp.where(cells[:, :LON] == offset, line, 0.0), axis=-1, keepdims=True)


def allowed_keys(num, pad, cells, keys):
    band, bands = lax.axis_index("sp"), lax.axis_size("sp")
    last = bands * LATW
    firsts = [lax.rem(band * LATW + last + by, last) for by in (-6, 0, 6, 12)]
    valid = [valid_cells(pad, cells, num[0], first) for first in firsts]
    row = lax.broadcasted_iota(jnp.int32, (WIN, WIN), 0)
    col = lax.broadcasted_iota(jnp.int32, (WIN, WIN), 1)
    apart = (row < PAD) != (col < PAD)
    for w, split in enumerate((band == 0, band == bands - 1)):
        at = slice(w * PAD, (w + 1) * PAD)
        real = jnp.concatenate([valid[2 * w][at], valid[2 * w + 1][at]], axis=0) > 0.5
        open_ = jnp.logical_not(apart & split)
        keys[w] = ((real & open_) | (row == col)).astype(F32)


def real_rows(axis):
    shape = (WIN, 1) if axis == 0 else (1, WIN)
    at = lax.broadcasted_iota(jnp.int32, shape, axis)
    return jnp.where(lax.rem(at, PAD) < PART, -1000000000.0, -3e38)


def head_masks():
    lane = lax.broadcasted_iota(jnp.int32, (1, PAIR), 1)
    return (lane < HEAD).astype(F32).astype(BF), (lane >= HEAD).astype(F32).astype(BF)


def softmax(scores, axis):
    expo = jnp.exp(scores - jnp.max(scores, axis=axis, keepdims=True))
    return expo * (1.0 / jnp.sum(expo, axis=axis, keepdims=True))


def window_copies(which, local, north, south, window, sems):
    pairs = (
        (north.at[which], window.at[pl.ds(0, PAD)]),
        (local.at[which], window.at[pl.ds(PAD, WIN)]),
        (south.at[which], window.at[pl.ds(PAD + WIN, PAD)]),
    )
    return [pltpu.make_async_copy(a, b, sems.at[i]) for i, (a, b) in enumerate(pairs)]


def weight_copies(weight, kept, sems):
    rows = weight.shape[0] // LOADS
    ats = [pl.ds(i * rows, rows) for i in range(LOADS)]
    return [pltpu.make_async_copy(weight.at[at], kept.at[at], sems.at[i]) for i, at in enumerate(ats)]


def start_all(copies):
    for copy in copies:
        copy.start()


def wait_all(copies):
    for copy in copies:
        copy.wait()


def columns(part, g):
    return slice((part * GROUPS + g) * GROUP, (part * GROUPS + g + 1) * GROUP)


def pack_all(window, kept, packed, loads):
    wait_all(loads)
    for g in range(GROUPS):
        for part in range(3):
            out = dot(window[...], kept[:, columns(part, g)])
            packed[:, columns(part, g)] = (out * HEAD**-0.5 if part == 0 else out).astype(BF)


def pair_at(part, w, p):
    start = part * HEADS * HEAD + p * PAIR
    return slice(w * WIN, (w + 1) * WIN), slice(start, start + PAIR)


def attend_kernel(
    num, local, north, south, pad, cells, weight, own, to_north, to_south,
    window, kept, packed, keys, wsem, ksem,
):
    moves = window_copies(0, local, north, south, window, wsem)
    loads = weight_copies(weight, kept, ksem)
    start_all(moves + loads)
    allowed_keys(num, pad, cells, keys)
    masks = head_masks()
    first = lax.broadcasted_iota(jnp.int32, (1, PAIR), 1) < HEAD
    low = real_rows(1)
    wait_all(moves)
    pack_all(window, kept, packed, loads)
    for w in range(2):
        ok = keys[w].T > 0.5
        for p in range(PAIRS):
            query, key, value = (packed[pair_at(part, w, p)] for part in range(3))
            mixed = []
            for mask in masks:
                scores = jnp.where(ok, dot_nt(query * mask, key), low)
                mixed.append(dot(softmax(scores, -1).astype(BF), value))
            out = jnp.where(first, mixed[0], mixed[1]).astype(BF)
            to = slice(p * PAIR, (p + 1) * PAIR)
            if w == 0:
                to_north[:, to] = out[:PAD]
                own[:PAD, to] = out[PAD:]
            else:
                own[PAD:, to] = out[:PAD]
                to_south[:, to] = out[PAD:]


def block_copies(blocks, raw, sems):
    planes = lax.axis_size("sp") // X_SIZE
    rows, width = raw.shape[0] // planes, raw.shape[1]
    plane = lax.div(lax.axis_index("sp"), X_SIZE)
    out = []
    for i, block in enumerate(blocks):
        j = min(i, planes // 2) if i <= planes // 2 + 1 else i - 1
        at = pl.ds(pl.multiple_of(lax.rem(plane + j, planes) * rows, rows), rows)
        to = raw.at[at] if block.shape[1] == width else raw.at[at, pl.ds((i - planes // 2) * width // 2, width // 2)]
        out.append(pltpu.make_async_copy(block, to, sems.at[i]))
    return out


def in_order(raw, wo):
    planes = lax.axis_size("sp") // X_SIZE
    rows = raw.shape[0] // planes
    turn = lax.rem(lax.axis_index("sp"), X_SIZE) * (rows // X_SIZE)
    row = lax.broadcasted_iota(jnp.int32, (rows, rows), 0)
    col = lax.broadcasted_iota(jnp.int32, (rows, rows), 1)
    place = (row == lax.rem(col + turn, rows)).astype(F32).astype(BF)
    for j in range(planes):
        at = slice(j * rows, (j + 1) * rows)
        wo[at] = dot(place, raw[at]).astype(BF)


def probs_kernel(
    num, local, north, south, pad, cells, weight, packed, probs, window, kept, keys, wsem, ksem
):
    moves = window_copies(1, local, north, south, window, wsem)
    loads = weight_copies(weight, kept, ksem)
    start_all(moves + loads)
    allowed_keys(num, pad, cells, keys)
    masks = head_masks()
    low = real_rows(0)
    wait_all(moves)
    pack_all(window, kept, packed, loads)
    for w in range(2):
        ok = keys[w] > 0.5
        for p in range(PAIRS):
            query, key = (packed[pair_at(part, w, p)] for part in range(2))
            for h, mask in enumerate(masks):
                scores = jnp.where(ok, dot_nt(key, query * mask), low)
                probs[w, 2 * p + h] = softmax(scores, 0).astype(BF)


def back_kernel(num, local, north, south, pad, cells, packed, probs, weight, *rest):
    blocks, rest = rest[:BLOCKS], rest[BLOCKS:]
    own, to_north, to_south, cot, kept, raw, wo, qkv, held, upstream, keys, grads, csem, ksem, osem, psem = rest
    cots = window_copies(2, local, north, south, cot, csem)
    loads = weight_copies(weight, kept, ksem)
    outs = block_copies(blocks, raw, osem)
    halves = [pltpu.make_async_copy(probs.at[w], held.at[w], psem.at[w]) for w in range(2)]
    halves.append(pltpu.make_async_copy(packed, qkv, psem.at[2]))
    start_all(outs + cots + halves + loads)
    allowed_keys(num, pad, cells, keys)
    masks = head_masks()
    first = lax.broadcasted_iota(jnp.int32, (1, PAIR), 1) < HEAD
    wait_all(outs)
    in_order(raw, wo)
    wait_all(cots)
    for g in range(GROUPS):
        at = slice(g * GROUP, (g + 1) * GROUP)
        upstream[:, at] = dot_nt(cot[...], wo[at, :]).astype(BF)
    wait_all(halves)
    for w in range(2):
        ok = keys[w] > 0.5
        for p in range(PAIRS):
            query, key, value = (qkv[pair_at(part, w, p)] for part in range(3))
            above = upstream[pair_at(0, w, p)]
            dq, dk, dv = [], [], []
            for h, mask in enumerate(masks):
                given = held[w, 2 * p + h]
                wide = given.astype(F32)
                g_probs = dot_nt(value, above * mask)
                inner = jnp.sum(wide * g_probs, axis=0, keepdims=True)
                g_scores = jnp.where(ok, wide * (g_probs - inner), 0.0).astype(BF)
                dq.append(dot_tn(g_scores, key))
                dk.append(dot(g_scores, query))
                dv.append(dot(given, above))
            for part, (pair, scale) in enumerate(((dq, HEAD**-0.5), (dk, 1.0), (dv, 1.0))):
                grads[pair_at(part, w, p)] = (jnp.where(first, pair[0], pair[1]) * scale).astype(BF)
    wait_all(loads)
    for n in range(0, own.shape[1], GROUP):
        out = dot_nt(grads[...], kept[n : n + GROUP, :]).astype(BF)
        to_north[:, n : n + GROUP] = out[:PAD]
        own[:, n : n + GROUP] = out[PAD : PAD + WIN]
        to_south[:, n : n + GROUP] = out[PAD + WIN :]


def half_in_order(place, north_part, south_part):
    return dot_tn(place, jnp.concatenate([north_part, south_part], axis=0))


def project_kernel(num, own, from_south, from_north, sec, mir, table, *rest):
    blocks, (out, raw, wo, sems) = rest[:BLOCKS], rest[BLOCKS:]
    outs = block_copies(blocks, raw, sems)
    start_all(outs)
    place = one_hot(table, num[0])
    top = half_in_order(place, own[:PAD], from_north[...]).astype(BF)
    low = half_in_order(place, from_south[...], own[PAD:]).astype(BF)
    mixed = jnp.concatenate([top, low], axis=0)
    decoder = is_decoder()
    wait_all(outs)
    in_order(raw, wo)
    for n in range(0, out.shape[2], GROUP):
        at = slice(n, n + GROUP)
        both = sec[:, :, at].reshape(2 * HALF, GROUP).astype(F32)
        both += decoder * mir[:, :, at].reshape(2 * HALF, GROUP).astype(F32)
        out[:, :, at] = (both + dot(mixed, wo[:, at])).astype(BF).reshape(-1, LEV, GROUP)


def norm_back_kernel(num, own, from_south, from_north, sav, grd, mir, gain, table, out):
    half = pl.program_id(0)
    place = one_hot(table, num[0])
    north_part = jnp.where(half == 0, own[...], from_south[...])
    south_part = jnp.where(half == 0, from_north[...], own[...])
    grad = half_in_order(place, north_part, south_part) * gain[...]
    centered, scale = norm_parts(tokens(sav).astype(F32))
    hat = centered * scale
    inner = jnp.mean(grad * hat, axis=-1, keepdims=True)
    through = scale * (grad - jnp.mean(grad, axis=-1, keepdims=True) - hat * inner)
    cot = (tokens(grd).astype(F32) + (1.0 - is_decoder()) * tokens(mir).astype(F32)).astype(BF)
    out[...] = (cot.astype(F32) + through).astype(BF).reshape(out.shape)


def shift(value, axis, by):
    peers = lax.axis_size(axis)
    return lax.ppermute(value, axis, [(i, (i + by) % peers) for i in range(peers)])


def mirrored(value, sources):
    peers = lax.axis_size("section")
    return lax.ppermute(value, "section", [(i, peers - 1 - i) for i in sources])


def along_x(value, by):
    peers = lax.axis_size("sp")
    return lax.ppermute(
        value, "sp", [(i, i // X_SIZE * X_SIZE + (i + by) % X_SIZE) for i in range(peers)]
    )


def along_z(value, by):
    return shift(value, "sp", by * X_SIZE)


def whole():
    return pl.BlockSpec(memory_space=pltpu.VMEM)


def call(kernel, out_shape, micros, **kw):
    return pl.pallas_call(
        kernel,
        out_shape=out_shape,
        compiler_params=pltpu.CompilerParams(vmem_limit_bytes=VMEM),
        cost_estimate=pl.CostEstimate(flops=int(micros * 10**9), bytes_accessed=2**20, transcendentals=0),
        **kw,
    )


def shards(
    section_input,
    mirror_input,
    saved_input,
    output_grad,
    qkv_weight,
    out_weight,
    norm_gain,
    land_bias,
    shift_offset,
    land_sea,
    pole_pad,
):
    sections = lax.axis_size("section")
    width = section_input.shape[-1]
    smem = pl.BlockSpec(memory_space=pltpu.SMEM)
    any_ = pl.BlockSpec(memory_space=pl.ANY)
    places, cells, spots = map(jnp.asarray, (place_table(), cell_table(), land_table()))

    def flat(value):
        return value[0].transpose(0, 2, 1, 3).reshape(LATW * LON, LEV, width)

    sec, mir, sav, grd = map(flat, (section_input, mirror_input, saved_input, output_grad))

    def like(*shape):
        return jax.ShapeDtypeStruct(shape, BF)

    def fixed(*shape):
        return pl.BlockSpec(shape, lambda i: (0,) * len(shape))

    half = pl.BlockSpec((LATW * LON // 2, LEV, width), lambda i: (i, 0, 0))
    local, down, up = call(
        prepare_kernel,
        (like(3, WIN, width), like(3, PAD, width), like(3, PAD, width)),
        5.0,
        grid=(2,),
        in_specs=[smem]
        + [half] * 4
        + [fixed(1, width)] * 2
        + [fixed(LATW, LON), fixed(*places.shape), fixed(*spots.shape)],
        out_specs=(
            pl.BlockSpec((3, PAD, width), lambda i: (0, i, 0)),
            fixed(3, PAD, width),
            fixed(3, PAD, width),
        ),
        name="prepare",
    )(shift_offset, sec, mir, sav, grd, norm_gain, land_bias, land_sea, places, spots)

    shard = out_weight[0]
    near = [along_x(shard, by) for by in (-1, 2, 1)]
    near, down, up = lax.optimization_barrier((near, down, up))
    line = jnp.concatenate([shard, *near], axis=0)
    ups, downs = [along_z(line, 1)], [along_z(line, -1)]
    north = shift(down, "sp", 1)
    south = shift(up, "sp", -1)
    ups.append(along_z(ups[-1], 1))
    downs.append(along_z(downs[-1], -1))
    weight = qkv_weight[0]
    inner = HEADS * HEAD
    dma = pltpu.SemaphoreType.DMA

    own, to_north, to_south = call(
        attend_kernel,
        (like(WIN, inner), like(PAD, inner), like(PAD, inner)),
        6.0,
        in_specs=[smem, any_, any_, any_, whole(), whole(), any_],
        out_specs=(whole(),) * 3,
        scratch_shapes=[
            pltpu.VMEM((2 * WIN, width), BF),
            pltpu.VMEM((width, 3 * inner), BF),
            pltpu.VMEM((2 * WIN, 3 * inner), BF),
            pltpu.VMEM((2, WIN, WIN), F32),
            dma((3,)),
            dma((LOADS,)),
        ],
        name="attend",
    )(shift_offset, local, north, south, pole_pad, cells, weight)
    from_south = shift(to_north, "sp", -1)
    from_north = shift(to_south, "sp", 1)
    above, below, own = lax.optimization_barrier((ups[-1], downs[-1], own))
    ups.append(along_z(above, 1))
    downs.append(along_z(below, -1))
    local, own = lax.optimization_barrier((local, own))
    packed, probs = call(
        probs_kernel,
        (like(2 * WIN, 3 * inner), like(2, HEADS, WIN, WIN)),
        6.0,
        in_specs=[smem, any_, any_, any_, whole(), whole(), any_],
        out_specs=(whole(),) * 2,
        scratch_shapes=[
            pltpu.VMEM((2 * WIN, width), BF),
            pltpu.VMEM((width, 3 * inner), BF),
            pltpu.VMEM((2, WIN, WIN), F32),
            dma((3,)),
            dma((LOADS,)),
        ],
        name="probs",
    )(shift_offset, local, north, south, pole_pad, cells, weight)
    above, below, probs = lax.optimization_barrier((ups[-1], downs[-1], probs))
    cut = width // 2
    ends = [along_z(above[:, :cut], 1), along_z(below[:, cut:], -1)]
    full = [line, *downs, *ends, *ups[::-1]]
    own_grad, grad_to_north, grad_to_south = call(
        back_kernel,
        (like(WIN, width), like(PAD, width), like(PAD, width)),
        15.0,
        in_specs=[smem, any_, any_, any_, whole(), whole()] + [any_] * (3 + BLOCKS),
        out_specs=(whole(),) * 3,
        scratch_shapes=[
            pltpu.VMEM((2 * WIN, width), BF),
            pltpu.VMEM((width, 3 * inner), BF),
            pltpu.VMEM((inner, width), BF),
            pltpu.VMEM((inner, width), BF),
            pltpu.VMEM((2 * WIN, 3 * inner), BF),
            pltpu.VMEM((2, HEADS, WIN, WIN), BF),
            pltpu.VMEM((2 * WIN, inner), BF),
            pltpu.VMEM((2, WIN, WIN), F32),
            pltpu.VMEM((2 * WIN, 3 * inner), BF),
            dma((3,)),
            dma((LOADS,)),
            dma((BLOCKS,)),
            dma((3,)),
        ],
        name="attend_back",
    )(shift_offset, local, north, south, pole_pad, cells, packed, probs, weight, *full)
    grad_from_south = shift(grad_to_north, "sp", -1)
    grad_from_north = shift(grad_to_south, "sp", 1)
    own, from_south, from_north, _ = lax.optimization_barrier((own, from_south, from_north, own_grad))
    block_out = call(
        project_kernel,
        like(LATW * LON, LEV, width),
        4.0,
        in_specs=[smem] + [whole()] * 6 + [any_] * BLOCKS,
        out_specs=whole(),
        scratch_shapes=[pltpu.VMEM((inner, width), BF), pltpu.VMEM((inner, width), BF), dma((BLOCKS,))],
        name="project",
    )(shift_offset, own, from_south, from_north, sec, mir, places, *full)
    grad_input = call(
        norm_back_kernel,
        like(LATW * LON, LEV, width),
        4.0,
        grid=(2,),
        in_specs=[smem, pl.BlockSpec((PAD, width), lambda i: (i, 0))]
        + [fixed(PAD, width)] * 2
        + [half] * 3
        + [fixed(1, width), fixed(*places.shape)],
        out_specs=half,
        name="norm_back",
    )(shift_offset, own_grad, grad_from_south, grad_from_north, sav, grd, mir, norm_gain, places)

    half_way = sections // 2
    forward = shift(block_out, "section", 1)
    skips = mirrored(block_out, range(half_way - 1))
    backward = shift(grad_input, "section", -1)
    skip_grads = mirrored(grad_input, range(half_way + 1, sections))
    section = lax.axis_index("section")
    mirror_out = jnp.where(
        section >= half_way,
        jnp.where(section == half_way, forward, skips),
        jnp.where(section == half_way - 1, backward, skip_grads),
    )

    def back(value):
        return value.reshape(LATW, LON, LEV, width).transpose(0, 2, 1, 3)[None]

    return back(forward), back(backward), back(mirror_out)


def solution(mesh):
    return jax.shard_map(
        shards,
        mesh=mesh,
        in_specs=(
            P("section", "sp", None, None, None),
            P("section", "sp", None, None, None),
            P("section", "sp", None, None, None),
            P("section", "sp", None, None, None),
            P("section", None, None),
            P("section", "sp", None),
            P("section", None),
            P("section", None),
            P("section"),
            P("sp", None),
            P(),
        ),
        out_specs=(
            P("section", "sp", None, None, None),
            P("section", "sp", None, None, None),
            P("section", "sp", None, None, None),
        ),
        check_vma=False,
    )
```

```python
import functools

import jax
import jax.numpy as jnp
import numpy as np
from jax import lax
from jax.experimental import pallas as pl
from jax.experimental.pallas import tpu as pltpu
from jax.sharding import PartitionSpec as P

HEADS = 12
HEAD = 64
LATW = 12
LONW = 6
LEV = 2
LON = 12
HALF = LATW // 2 * LEV * LON
PART = HALF // 2
PAD = 80
WIN = 2 * PAD
PAIR = 2 * HEAD
PAIRS = HEADS // 2
GROUP = 2 * PAIR
X_SIZE = 4
BLOCKS = 9
LOADS = 12
GROUPS = HEADS * HEAD // GROUP
BF = jnp.bfloat16
F32 = jnp.float32
VMEM = 60 * 2**20


def row_parts():
    rows = np.arange(WIN)
    side, within = rows // PAD, rows % PAD
    spot = side * LONW + within % (LONW * LEV) // LEV
    return within < PART, within // (LONW * LEV), spot, within % LEV


def place_table():
    real, lat, spot, level = (part[:, None] for part in row_parts())
    token = np.arange(HALF)[None, :]
    same = real & (lat == token // (LON * LEV)) & (level == token % LEV)
    return np.where(same, (token // LEV % LON - spot) % LON, -1).astype(np.int32)


def cell_table():
    real, lat, spot, _ = (part[:, None] for part in row_parts())
    shifts = np.where(real, (np.arange(LON)[None, :] - spot) % LON, -1)
    return np.concatenate([shifts, lat], axis=1).astype(np.int32)


def land_table():
    token = np.arange(HALF)[:, None]
    return np.concatenate([token // (LON * LEV), token // LEV % LON], axis=1).astype(np.int32)


def dot(a, b):
    return jnp.dot(a, b, preferred_element_type=F32)


def dot_nt(a, b):
    return lax.dot_general(a, b, (((1,), (1,)), ((), ())), preferred_element_type=F32)


def dot_tn(a, b):
    return lax.dot_general(a, b, (((0,), (0,)), ((), ())), preferred_element_type=F32)


def one_hot(table_ref, offset):
    return (table_ref[...] == offset).astype(F32).astype(BF)


def is_decoder():
    return (lax.axis_index("section") >= lax.axis_size("section") // 2).astype(F32)


def tokens(ref):
    return ref[...].reshape(-1, ref.shape[-1])


def norm_parts(rows):
    centered = rows - jnp.mean(rows, axis=-1, keepdims=True)
    spread = jnp.mean(centered * centered, axis=-1, keepdims=True)
    return centered, lax.rsqrt(spread + 1e-05)


def spread(half, place, arrays, local, down, up):
    for i, rows in enumerate(arrays):
        placed = dot(place, rows).astype(BF)

        @pl.when(half == 0)
        def _():
            local[i] = placed[:PAD]
            up[i] = placed[PAD:]

        @pl.when(half == 1)
        def _():
            local[i] = placed[PAD:]
            down[i] = placed[:PAD]


def normed(rows, gain, bias, land, where):
    half = pl.program_id(0)
    lat, lon = where[:, 0:1], where[:, 1:2]
    cells = land[...].astype(F32)
    line = jnp.zeros((HALF, LON), F32)
    for row in range(LATW // 2):
        both = jnp.where(half == 0, cells[row : row + 1], cells[row + LATW // 2 : row + LATW // 2 + 1])
        line = jnp.where(lat == row, both, line)
    spots = lax.broadcasted_iota(jnp.int32, (HALF, LON), 1) == lon
    on_land = jnp.sum(jnp.where(spots, line, 0.0), axis=-1, keepdims=True)
    centered, scale = norm_parts(rows)
    return (centered * scale * gain[...] + on_land * bias[...]).astype(BF)


def prepare_kernel(num, sec, mir, gain, bias, land, table, where, local, down, up):
    start = tokens(sec).astype(F32) + is_decoder() * tokens(mir).astype(F32)
    rows = normed(start, gain, bias, land, where)
    spread(pl.program_id(0), one_hot(table, num[0]), [rows], local, down, up)


def prepare_back_kernel(num, sav, grd, mir, gain, bias, land, table, where, local, down, up):
    rows = normed(tokens(sav).astype(F32), gain, bias, land, where)
    cot = tokens(grd).astype(F32) + (1.0 - is_decoder()) * tokens(mir).astype(F32)
    spread(pl.program_id(0), one_hot(table, num[0]), [rows, cot.astype(BF)], local, down, up)


def valid_cells(pad, cells, offset, first_row):
    lat = cells[:, LON : LON + 1]
    line = jnp.zeros((WIN, LON), F32)
    for row in range(LATW // 2):
        line = jnp.where(lat == row, pad[pl.ds(first_row + row, 1), :].astype(F32), line)
    return jnp.max(jnp.where(cells[:, :LON] == offset, line, 0.0), axis=-1, keepdims=True)


def allowed_keys(num, pad, cells, keys):
    band, bands = lax.axis_index("sp"), lax.axis_size("sp")
    last = bands * LATW
    firsts = [lax.rem(band * LATW + last + by, last) for by in (-6, 0, 6, 12)]
    valid = [valid_cells(pad, cells, num[0], first) for first in firsts]
    row = lax.broadcasted_iota(jnp.int32, (WIN, WIN), 0)
    col = lax.broadcasted_iota(jnp.int32, (WIN, WIN), 1)
    apart = (row < PAD) != (col < PAD)
    for w, split in enumerate((band == 0, band == bands - 1)):
        at = slice(w * PAD, (w + 1) * PAD)
        real = jnp.concatenate([valid[2 * w][at], valid[2 * w + 1][at]], axis=0) > 0.5
        open_ = jnp.logical_not(apart & split)
        keys[w] = ((real & open_) | (row == col)).astype(F32)


def real_rows(axis):
    shape = (WIN, 1) if axis == 0 else (1, WIN)
    at = lax.broadcasted_iota(jnp.int32, shape, axis)
    return jnp.where(lax.rem(at, PAD) < PART, -1000000000.0, -3e38)


def head_masks():
    lane = lax.broadcasted_iota(jnp.int32, (1, PAIR), 1)
    return (lane < HEAD).astype(F32).astype(BF), (lane >= HEAD).astype(F32).astype(BF)


def softmax(scores, axis):
    expo = jnp.exp(scores - jnp.max(scores, axis=axis, keepdims=True))
    return expo * (1.0 / jnp.sum(expo, axis=axis, keepdims=True))


def window_copies(which, local, north, south, window, sems):
    pairs = (
        (north.at[which], window.at[pl.ds(0, PAD)]),
        (local.at[which], window.at[pl.ds(PAD, WIN)]),
        (south.at[which], window.at[pl.ds(PAD + WIN, PAD)]),
    )
    return [pltpu.make_async_copy(a, b, sems.at[i]) for i, (a, b) in enumerate(pairs)]


def weight_copies(weight, kept, sems):
    rows = weight.shape[0] // LOADS
    ats = [pl.ds(i * rows, rows) for i in range(LOADS)]
    return [pltpu.make_async_copy(weight.at[at], kept.at[at], sems.at[i]) for i, at in enumerate(ats)]


def start_all(copies):
    for copy in copies:
        copy.start()


def wait_all(copies):
    for copy in copies:
        copy.wait()


def columns(part, g):
    return slice((part * GROUPS + g) * GROUP, (part * GROUPS + g + 1) * GROUP)


def pack_all(window, kept, packed, loads):
    wait_all(loads)
    for g in range(GROUPS):
        for part in range(3):
            out = dot(window[...], kept[:, columns(part, g)])
            packed[:, columns(part, g)] = (out * HEAD**-0.5 if part == 0 else out).astype(BF)


def pair_at(part, w, p):
    start = part * HEADS * HEAD + p * PAIR
    return slice(w * WIN, (w + 1) * WIN), slice(start, start + PAIR)


def attend_kernel(
    num, local, north, south, pad, cells, weight, own, to_north, to_south,
    window, kept, packed, keys, wsem, ksem,
):
    moves = window_copies(0, local, north, south, window, wsem)
    loads = weight_copies(weight, kept, ksem)
    start_all(moves + loads)
    allowed_keys(num, pad, cells, keys)
    masks = head_masks()
    first = lax.broadcasted_iota(jnp.int32, (1, PAIR), 1) < HEAD
    low = real_rows(1)
    wait_all(moves)
    pack_all(window, kept, packed, loads)
    for w in range(2):
        ok = keys[w].T > 0.5
        for p in range(PAIRS):
            query, key, value = (packed[pair_at(part, w, p)] for part in range(3))
            mixed = []
            for mask in masks:
                scores = jnp.where(ok, dot_nt(query * mask, key), low)
                mixed.append(dot(softmax(scores, -1).astype(BF), value))
            out = jnp.where(first, mixed[0], mixed[1]).astype(BF)
            to = slice(p * PAIR, (p + 1) * PAIR)
            if w == 0:
                to_north[:, to] = out[:PAD]
                own[:PAD, to] = out[PAD:]
            else:
                own[PAD:, to] = out[:PAD]
                to_south[:, to] = out[PAD:]


def block_copies(blocks, raw, sems):
    planes = lax.axis_size("sp") // X_SIZE
    rows, width = raw.shape[0] // planes, raw.shape[1]
    plane = lax.div(lax.axis_index("sp"), X_SIZE)
    out = []
    for i, block in enumerate(blocks):
        j = min(i, planes // 2) if i <= planes // 2 + 1 else i - 1
        at = pl.ds(pl.multiple_of(lax.rem(plane + j, planes) * rows, rows), rows)
        to = raw.at[at] if block.shape[1] == width else raw.at[at, pl.ds((i - planes // 2) * width // 2, width // 2)]
        out.append(pltpu.make_async_copy(block, to, sems.at[i]))
    return out


def in_order(raw, wo):
    planes = lax.axis_size("sp") // X_SIZE
    rows = raw.shape[0] // planes
    turn = lax.rem(lax.axis_index("sp"), X_SIZE) * (rows // X_SIZE)
    row = lax.broadcasted_iota(jnp.int32, (rows, rows), 0)
    col = lax.broadcasted_iota(jnp.int32, (rows, rows), 1)
    place = (row == lax.rem(col + turn, rows)).astype(F32).astype(BF)
    for j in range(planes):
        at = slice(j * rows, (j + 1) * rows)
        wo[at] = dot(place, raw[at]).astype(BF)


def probs_kernel(
    num, local, north, south, pad, cells, weight, packed, probs, window, kept, keys, wsem, ksem
):
    moves = window_copies(0, local, north, south, window, wsem)
    loads = weight_copies(weight, kept, ksem)
    start_all(moves + loads)
    allowed_keys(num, pad, cells, keys)
    masks = head_masks()
    low = real_rows(0)
    wait_all(moves)
    pack_all(window, kept, packed, loads)
    for w in range(2):
        ok = keys[w] > 0.5
        for p in range(PAIRS):
            query, key = (packed[pair_at(part, w, p)] for part in range(2))
            for h, mask in enumerate(masks):
                scores = jnp.where(ok, dot_nt(key, query * mask), low)
                probs[w, 2 * p + h] = softmax(scores, 0).astype(BF)


def back_kernel(num, local, north, south, pad, cells, packed, probs, weight, *rest):
    blocks, rest = rest[:BLOCKS], rest[BLOCKS:]
    own, to_north, to_south, cot, kept, raw, wo, qkv, held, upstream, keys, grads, csem, ksem, osem, psem = rest
    cots = window_copies(1, local, north, south, cot, csem)
    loads = weight_copies(weight, kept, ksem)
    outs = block_copies(blocks, raw, osem)
    halves = [pltpu.make_async_copy(probs.at[w], held.at[w], psem.at[w]) for w in range(2)]
    halves.append(pltpu.make_async_copy(packed, qkv, psem.at[2]))
    start_all(outs + cots + halves)
    allowed_keys(num, pad, cells, keys)
    masks = head_masks()
    first = lax.broadcasted_iota(jnp.int32, (1, PAIR), 1) < HEAD
    wait_all(outs + cots)
    start_all(loads)
    in_order(raw, wo)
    for g in range(GROUPS):
        at = slice(g * GROUP, (g + 1) * GROUP)
        upstream[:, at] = dot_nt(cot[...], wo[at, :]).astype(BF)
    wait_all(halves)
    for w in range(2):
        ok = keys[w] > 0.5
        for p in range(PAIRS):
            query, key, value = (qkv[pair_at(part, w, p)] for part in range(3))
            above = upstream[pair_at(0, w, p)]
            dq, dk, dv = [], [], []
            for h, mask in enumerate(masks):
                given = held[w, 2 * p + h]
                wide = given.astype(F32)
                g_probs = dot_nt(value, above * mask)
                inner = jnp.sum(wide * g_probs, axis=0, keepdims=True)
                g_scores = jnp.where(ok, wide * (g_probs - inner), 0.0).astype(BF)
                dq.append(dot_tn(g_scores, key))
                dk.append(dot(g_scores, query))
                dv.append(dot(given, above))
            for part, (pair, scale) in enumerate(((dq, HEAD**-0.5), (dk, 1.0), (dv, 1.0))):
                grads[pair_at(part, w, p)] = (jnp.where(first, pair[0], pair[1]) * scale).astype(BF)
    wait_all(loads)
    for n in range(0, own.shape[1], GROUP):
        out = dot_nt(grads[...], kept[n : n + GROUP, :]).astype(BF)
        to_north[:, n : n + GROUP] = out[:PAD]
        own[:, n : n + GROUP] = out[PAD : PAD + WIN]
        to_south[:, n : n + GROUP] = out[PAD + WIN :]


def half_in_order(place, north_part, south_part):
    return dot_tn(place, jnp.concatenate([north_part, south_part], axis=0))


def project_kernel(num, own, from_south, from_north, sec, mir, table, *rest):
    blocks, (out, raw, wo, sems) = rest[:BLOCKS], rest[BLOCKS:]
    outs = block_copies(blocks, raw, sems)
    start_all(outs)
    place = one_hot(table, num[0])
    top = half_in_order(place, own[:PAD], from_north[...]).astype(BF)
    low = half_in_order(place, from_south[...], own[PAD:]).astype(BF)
    mixed = jnp.concatenate([top, low], axis=0)
    decoder = is_decoder()
    wait_all(outs)
    in_order(raw, wo)
    for n in range(0, out.shape[2], GROUP):
        at = slice(n, n + GROUP)
        both = sec[:, :, at].reshape(2 * HALF, GROUP).astype(F32)
        both += decoder * mir[:, :, at].reshape(2 * HALF, GROUP).astype(F32)
        out[:, :, at] = (both + dot(mixed, wo[:, at])).astype(BF).reshape(-1, LEV, GROUP)


def norm_back_kernel(num, own, from_south, from_north, sav, grd, mir, gain, table, out):
    half = pl.program_id(0)
    place = one_hot(table, num[0])
    north_part = jnp.where(half == 0, own[...], from_south[...])
    south_part = jnp.where(half == 0, from_north[...], own[...])
    grad = half_in_order(place, north_part, south_part) * gain[...]
    centered, scale = norm_parts(tokens(sav).astype(F32))
    hat = centered * scale
    inner = jnp.mean(grad * hat, axis=-1, keepdims=True)
    through = scale * (grad - jnp.mean(grad, axis=-1, keepdims=True) - hat * inner)
    cot = (tokens(grd).astype(F32) + (1.0 - is_decoder()) * tokens(mir).astype(F32)).astype(BF)
    out[...] = (cot.astype(F32) + through).astype(BF).reshape(out.shape)


def shift(value, axis, by):
    peers = lax.axis_size(axis)
    return lax.ppermute(value, axis, [(i, (i + by) % peers) for i in range(peers)])


def mirrored(value, sources):
    peers = lax.axis_size("section")
    return lax.ppermute(value, "section", [(i, peers - 1 - i) for i in sources])


def along_x(value, by):
    peers = lax.axis_size("sp")
    return lax.ppermute(
        value, "sp", [(i, i // X_SIZE * X_SIZE + (i + by) % X_SIZE) for i in range(peers)]
    )


def along_z(value, by):
    return shift(value, "sp", by * X_SIZE)


def whole():
    return pl.BlockSpec(memory_space=pltpu.VMEM)


def call(kernel, out_shape, micros, **kw):
    return pl.pallas_call(
        kernel,
        out_shape=out_shape,
        compiler_params=pltpu.CompilerParams(vmem_limit_bytes=VMEM),
        cost_estimate=pl.CostEstimate(flops=int(micros * 10**9), bytes_accessed=2**20, transcendentals=0),
        **kw,
    )


def shards(
    section_input,
    mirror_input,
    saved_input,
    output_grad,
    qkv_weight,
    out_weight,
    norm_gain,
    land_bias,
    shift_offset,
    land_sea,
    pole_pad,
):
    sections = lax.axis_size("section")
    width = section_input.shape[-1]
    smem = pl.BlockSpec(memory_space=pltpu.SMEM)
    any_ = pl.BlockSpec(memory_space=pl.ANY)
    places, cells, spots = map(jnp.asarray, (place_table(), cell_table(), land_table()))

    def flat(value):
        return value[0].transpose(0, 2, 1, 3).reshape(LATW * LON, LEV, width)

    sec, mir, sav, grd = map(flat, (section_input, mirror_input, saved_input, output_grad))

    def like(*shape):
        return jax.ShapeDtypeStruct(shape, BF)

    def fixed(*shape):
        return pl.BlockSpec(shape, lambda i: (0,) * len(shape))

    half = pl.BlockSpec((LATW * LON // 2, LEV, width), lambda i: (i, 0, 0))

    def prepared(kernel, arrays, count, name):
        return call(
            kernel,
            (like(count, WIN, width), like(count, PAD, width), like(count, PAD, width)),
            4.0,
            grid=(2,),
            in_specs=[smem]
            + [half] * len(arrays)
            + [fixed(1, width)] * 2
            + [fixed(LATW, LON), fixed(*places.shape), fixed(*spots.shape)],
            out_specs=(
                pl.BlockSpec((count, PAD, width), lambda i: (0, i, 0)),
                fixed(count, PAD, width),
                fixed(count, PAD, width),
            ),
            name=name,
        )(shift_offset, *arrays, norm_gain, land_bias, land_sea, places, spots)

    shard = out_weight[0]
    near = [along_x(shard, by) for by in (-1, 2, 1)]
    local, down, up = prepared(prepare_kernel, (sec, mir), 1, "prepare")
    near, down, up = lax.optimization_barrier((near, down, up))
    line = jnp.concatenate([shard, *near], axis=0)
    north = shift(down, "sp", 1)
    south = shift(up, "sp", -1)
    ups, downs = [along_z(line, 1)], [along_z(line, -1)]
    sav, line = lax.optimization_barrier((sav, line))
    local_back, down, up = prepared(prepare_back_kernel, (sav, grd, mir), 2, "prepare_back")
    north_back = shift(down, "sp", 1)
    south_back = shift(up, "sp", -1)
    ups.append(along_z(ups[-1], 1))
    downs.append(along_z(downs[-1], -1))
    weight = qkv_weight[0]
    inner = HEADS * HEAD
    dma = pltpu.SemaphoreType.DMA

    own, to_north, to_south = call(
        attend_kernel,
        (like(WIN, inner), like(PAD, inner), like(PAD, inner)),
        6.0,
        in_specs=[smem, any_, any_, any_, whole(), whole(), any_],
        out_specs=(whole(),) * 3,
        scratch_shapes=[
            pltpu.VMEM((2 * WIN, width), BF),
            pltpu.VMEM((width, 3 * inner), BF),
            pltpu.VMEM((2 * WIN, 3 * inner), BF),
            pltpu.VMEM((2, WIN, WIN), F32),
            dma((3,)),
            dma((LOADS,)),
        ],
        name="attend",
    )(shift_offset, local, north, south, pole_pad, cells, weight)
    from_south = shift(to_north, "sp", -1)
    from_north = shift(to_south, "sp", 1)
    above, below, own = lax.optimization_barrier((ups[-1], downs[-1], own))
    ups.append(along_z(above, 1))
    downs.append(along_z(below, -1))
    local_back, own = lax.optimization_barrier((local_back, own))
    packed, probs = call(
        probs_kernel,
        (like(2 * WIN, 3 * inner), like(2, HEADS, WIN, WIN)),
        6.0,
        in_specs=[smem, any_, any_, any_, whole(), whole(), any_],
        out_specs=(whole(),) * 2,
        scratch_shapes=[
            pltpu.VMEM((2 * WIN, width), BF),
            pltpu.VMEM((width, 3 * inner), BF),
            pltpu.VMEM((2, WIN, WIN), F32),
            dma((3,)),
            dma((LOADS,)),
        ],
        name="probs",
    )(shift_offset, local_back, north_back, south_back, pole_pad, cells, weight)
    above, below, probs = lax.optimization_barrier((ups[-1], downs[-1], probs))
    cut = width // 2
    ends = [along_z(above[:, :cut], 1), along_z(below[:, cut:], -1)]
    full = [line, *downs, *ends, *ups[::-1]]
    own_grad, grad_to_north, grad_to_south = call(
        back_kernel,
        (like(WIN, width), like(PAD, width), like(PAD, width)),
        15.0,
        in_specs=[smem, any_, any_, any_, whole(), whole()] + [any_] * (3 + BLOCKS),
        out_specs=(whole(),) * 3,
        scratch_shapes=[
            pltpu.VMEM((2 * WIN, width), BF),
            pltpu.VMEM((width, 3 * inner), BF),
            pltpu.VMEM((inner, width), BF),
            pltpu.VMEM((inner, width), BF),
            pltpu.VMEM((2 * WIN, 3 * inner), BF),
            pltpu.VMEM((2, HEADS, WIN, WIN), BF),
            pltpu.VMEM((2 * WIN, inner), BF),
            pltpu.VMEM((2, WIN, WIN), F32),
            pltpu.VMEM((2 * WIN, 3 * inner), BF),
            dma((3,)),
            dma((LOADS,)),
            dma((BLOCKS,)),
            dma((3,)),
        ],
        name="attend_back",
    )(shift_offset, local_back, north_back, south_back, pole_pad, cells, packed, probs, weight, *full)
    grad_from_south = shift(grad_to_north, "sp", -1)
    grad_from_north = shift(grad_to_south, "sp", 1)
    own, from_south, from_north, _ = lax.optimization_barrier((own, from_south, from_north, own_grad))
    block_out = call(
        project_kernel,
        like(LATW * LON, LEV, width),
        4.0,
        in_specs=[smem] + [whole()] * 6 + [any_] * BLOCKS,
        out_specs=whole(),
        scratch_shapes=[pltpu.VMEM((inner, width), BF), pltpu.VMEM((inner, width), BF), dma((BLOCKS,))],
        name="project",
    )(shift_offset, own, from_south, from_north, sec, mir, places, *full)
    grad_input = call(
        norm_back_kernel,
        like(LATW * LON, LEV, width),
        4.0,
        grid=(2,),
        in_specs=[smem, pl.BlockSpec((PAD, width), lambda i: (i, 0))]
        + [fixed(PAD, width)] * 2
        + [half] * 3
        + [fixed(1, width), fixed(*places.shape)],
        out_specs=half,
        name="norm_back",
    )(shift_offset, own_grad, grad_from_south, grad_from_north, sav, grd, mir, norm_gain, places)

    half_way = sections // 2
    forward = shift(block_out, "section", 1)
    skips = mirrored(block_out, range(half_way - 1))
    backward = shift(grad_input, "section", -1)
    skip_grads = mirrored(grad_input, range(half_way + 1, sections))
    section = lax.axis_index("section")
    mirror_out = jnp.where(
        section >= half_way,
        jnp.where(section == half_way, forward, skips),
        jnp.where(section == half_way - 1, backward, skip_grads),
    )

    def back(value):
        return value.reshape(LATW, LON, LEV, width).transpose(0, 2, 1, 3)[None]

    return back(forward), back(backward), back(mirror_out)


def solution(mesh):
    return jax.shard_map(
        shards,
        mesh=mesh,
        in_specs=(
            P("section", "sp", None, None, None),
            P("section", "sp", None, None, None),
            P("section", "sp", None, None, None),
            P("section", "sp", None, None, None),
            P("section", None, None),
            P("section", "sp", None),
            P("section", None),
            P("section", None),
            P("section"),
            P("sp", None),
            P(),
        ),
        out_specs=(
            P("section", "sp", None, None, None),
            P("section", "sp", None, None, None),
            P("section", "sp", None, None, None),
        ),
        check_vma=False,
    )
```

```python
import functools

import jax
import jax.numpy as jnp
import numpy as np
from jax import lax
from jax.experimental import pallas as pl
from jax.experimental.pallas import tpu as pltpu
from jax.sharding import PartitionSpec as P

HEADS = 12
HEAD = 64
LATW = 12
LONW = 6
LEV = 2
LON = 12
HALF = LATW // 2 * LEV * LON
PART = HALF // 2
PAD = 80
WIN = 2 * PAD
PAIR = 2 * HEAD
PAIRS = HEADS // 2
GROUP = 2 * PAIR
X_SIZE = 4
BLOCKS = 9
LOADS = 12
GROUPS = HEADS * HEAD // GROUP
BF = jnp.bfloat16
F32 = jnp.float32
VMEM = 60 * 2**20


def row_parts():
    rows = np.arange(WIN)
    side, within = rows // PAD, rows % PAD
    spot = side * LONW + within % (LONW * LEV) // LEV
    return within < PART, within // (LONW * LEV), spot, within % LEV


def place_table():
    real, lat, spot, level = (part[:, None] for part in row_parts())
    token = np.arange(HALF)[None, :]
    same = real & (lat == token // (LON * LEV)) & (level == token % LEV)
    return np.where(same, (token // LEV % LON - spot) % LON, -1).astype(np.int32)


def cell_table():
    real, lat, spot, _ = (part[:, None] for part in row_parts())
    shifts = np.where(real, (np.arange(LON)[None, :] - spot) % LON, -1)
    return np.concatenate([shifts, lat], axis=1).astype(np.int32)


def land_table():
    token = np.arange(HALF)[:, None]
    return np.concatenate([token // (LON * LEV), token // LEV % LON], axis=1).astype(np.int32)


def dot(a, b):
    return jnp.dot(a, b, preferred_element_type=F32)


def dot_nt(a, b):
    return lax.dot_general(a, b, (((1,), (1,)), ((), ())), preferred_element_type=F32)


def dot_tn(a, b):
    return lax.dot_general(a, b, (((0,), (0,)), ((), ())), preferred_element_type=F32)


def one_hot(table_ref, offset):
    return (table_ref[...] == offset).astype(F32).astype(BF)


def is_decoder():
    return (lax.axis_index("section") >= lax.axis_size("section") // 2).astype(F32)


def tokens(ref):
    return ref[...].reshape(-1, ref.shape[-1])


def norm_parts(rows):
    centered = rows - jnp.mean(rows, axis=-1, keepdims=True)
    spread = jnp.mean(centered * centered, axis=-1, keepdims=True)
    return centered, lax.rsqrt(spread + 1e-05)


def spread(half, place, arrays, local, down, up):
    for i, rows in enumerate(arrays):
        placed = dot(place, rows).astype(BF)

        @pl.when(half == 0)
        def _():
            local[i] = placed[:PAD]
            up[i] = placed[PAD:]

        @pl.when(half == 1)
        def _():
            local[i] = placed[PAD:]
            down[i] = placed[:PAD]


def normed(rows, gain, bias, land, where):
    half = pl.program_id(0)
    lat, lon = where[:, 0:1], where[:, 1:2]
    cells = land[...].astype(F32)
    line = jnp.zeros((HALF, LON), F32)
    for row in range(LATW // 2):
        both = jnp.where(half == 0, cells[row : row + 1], cells[row + LATW // 2 : row + LATW // 2 + 1])
        line = jnp.where(lat == row, both, line)
    spots = lax.broadcasted_iota(jnp.int32, (HALF, LON), 1) == lon
    on_land = jnp.sum(jnp.where(spots, line, 0.0), axis=-1, keepdims=True)
    centered, scale = norm_parts(rows)
    return (centered * scale * gain[...] + on_land * bias[...]).astype(BF)


def prepare_kernel(num, sec, mir, gain, bias, land, table, where, local, down, up):
    start = tokens(sec).astype(F32) + is_decoder() * tokens(mir).astype(F32)
    rows = normed(start, gain, bias, land, where)
    spread(pl.program_id(0), one_hot(table, num[0]), [rows], local, down, up)


def prepare_back_kernel(num, sav, grd, mir, gain, bias, land, table, where, local, down, up):
    rows = normed(tokens(sav).astype(F32), gain, bias, land, where)
    cot = tokens(grd).astype(F32) + (1.0 - is_decoder()) * tokens(mir).astype(F32)
    spread(pl.program_id(0), one_hot(table, num[0]), [rows, cot.astype(BF)], local, down, up)


def valid_cells(pad, cells, offset, first_row):
    lat = cells[:, LON : LON + 1]
    line = jnp.zeros((WIN, LON), F32)
    for row in range(LATW // 2):
        line = jnp.where(lat == row, pad[pl.ds(first_row + row, 1), :].astype(F32), line)
    return jnp.max(jnp.where(cells[:, :LON] == offset, line, 0.0), axis=-1, keepdims=True)


def allowed_keys(num, pad, cells, keys):
    band, bands = lax.axis_index("sp"), lax.axis_size("sp")
    last = bands * LATW
    firsts = [lax.rem(band * LATW + last + by, last) for by in (-6, 0, 6, 12)]
    valid = [valid_cells(pad, cells, num[0], first) for first in firsts]
    row = lax.broadcasted_iota(jnp.int32, (WIN, WIN), 0)
    col = lax.broadcasted_iota(jnp.int32, (WIN, WIN), 1)
    apart = (row < PAD) != (col < PAD)
    for w, split in enumerate((band == 0, band == bands - 1)):
        at = slice(w * PAD, (w + 1) * PAD)
        real = jnp.concatenate([valid[2 * w][at], valid[2 * w + 1][at]], axis=0) > 0.5
        open_ = jnp.logical_not(apart & split)
        keys[w] = ((real & open_) | (row == col)).astype(F32)


def real_rows(axis):
    shape = (WIN, 1) if axis == 0 else (1, WIN)
    at = lax.broadcasted_iota(jnp.int32, shape, axis)
    return jnp.where(lax.rem(at, PAD) < PART, -1000000000.0, -3e38)


def head_masks():
    lane = lax.broadcasted_iota(jnp.int32, (1, PAIR), 1)
    return (lane < HEAD).astype(F32).astype(BF), (lane >= HEAD).astype(F32).astype(BF)


def softmax(scores, axis):
    expo = jnp.exp(scores - jnp.max(scores, axis=axis, keepdims=True))
    return expo * (1.0 / jnp.sum(expo, axis=axis, keepdims=True))


def window_copies(which, local, north, south, window, sems):
    pairs = (
        (north.at[which], window.at[pl.ds(0, PAD)]),
        (local.at[which], window.at[pl.ds(PAD, WIN)]),
        (south.at[which], window.at[pl.ds(PAD + WIN, PAD)]),
    )
    return [pltpu.make_async_copy(a, b, sems.at[i]) for i, (a, b) in enumerate(pairs)]


def weight_copies(weight, kept, sems):
    rows = weight.shape[0] // LOADS
    ats = [pl.ds(i * rows, rows) for i in range(LOADS)]
    return [pltpu.make_async_copy(weight.at[at], kept.at[at], sems.at[i]) for i, at in enumerate(ats)]


def start_all(copies):
    for copy in copies:
        copy.start()


def wait_all(copies):
    for copy in copies:
        copy.wait()


def columns(part, g):
    return slice((part * GROUPS + g) * GROUP, (part * GROUPS + g + 1) * GROUP)


def pack_all(window, kept, packed, loads):
    wait_all(loads)
    for g in range(GROUPS):
        for part in range(3):
            out = dot(window[...], kept[:, columns(part, g)])
            packed[:, columns(part, g)] = (out * HEAD**-0.5 if part == 0 else out).astype(BF)


def pair_at(part, w, p):
    start = part * HEADS * HEAD + p * PAIR
    return slice(w * WIN, (w + 1) * WIN), slice(start, start + PAIR)


def attend_kernel(
    num, local, north, south, pad, cells, weight, own, to_north, to_south,
    window, kept, packed, keys, wsem, ksem,
):
    moves = window_copies(0, local, north, south, window, wsem)
    loads = weight_copies(weight, kept, ksem)
    start_all(moves + loads)
    allowed_keys(num, pad, cells, keys)
    masks = head_masks()
    first = lax.broadcasted_iota(jnp.int32, (1, PAIR), 1) < HEAD
    low = real_rows(1)
    wait_all(moves)
    pack_all(window, kept, packed, loads)
    for w in range(2):
        ok = keys[w].T > 0.5
        for p in range(PAIRS):
            query, key, value = (packed[pair_at(part, w, p)] for part in range(3))
            mixed = []
            for mask in masks:
                scores = jnp.where(ok, dot_nt(query * mask, key), low)
                mixed.append(dot(softmax(scores, -1).astype(BF), value))
            out = jnp.where(first, mixed[0], mixed[1]).astype(BF)
            to = slice(p * PAIR, (p + 1) * PAIR)
            if w == 0:
                to_north[:, to] = out[:PAD]
                own[:PAD, to] = out[PAD:]
            else:
                own[PAD:, to] = out[:PAD]
                to_south[:, to] = out[PAD:]


def block_copies(blocks, raw, sems):
    planes = lax.axis_size("sp") // X_SIZE
    rows, width = raw.shape[0] // planes, raw.shape[1]
    plane = lax.div(lax.axis_index("sp"), X_SIZE)
    out = []
    for i, block in enumerate(blocks):
        j = min(i, planes // 2) if i <= planes // 2 + 1 else i - 1
        at = pl.ds(pl.multiple_of(lax.rem(plane + j, planes) * rows, rows), rows)
        to = raw.at[at] if block.shape[1] == width else raw.at[at, pl.ds((i - planes // 2) * width // 2, width // 2)]
        out.append(pltpu.make_async_copy(block, to, sems.at[i]))
    return out


def in_order(raw, wo):
    planes = lax.axis_size("sp") // X_SIZE
    rows = raw.shape[0] // planes
    turn = lax.rem(lax.axis_index("sp"), X_SIZE) * (rows // X_SIZE)
    row = lax.broadcasted_iota(jnp.int32, (rows, rows), 0)
    col = lax.broadcasted_iota(jnp.int32, (rows, rows), 1)
    place = (row == lax.rem(col + turn, rows)).astype(F32).astype(BF)
    for j in range(planes):
        at = slice(j * rows, (j + 1) * rows)
        wo[at] = dot(place, raw[at]).astype(BF)


def probs_kernel(
    num, local, north, south, pad, cells, weight, packed, probs, window, kept, keys, wsem, ksem
):
    moves = window_copies(0, local, north, south, window, wsem)
    loads = weight_copies(weight, kept, ksem)
    start_all(moves + loads)
    allowed_keys(num, pad, cells, keys)
    masks = head_masks()
    low = real_rows(0)
    wait_all(moves)
    pack_all(window, kept, packed, loads)
    for w in range(2):
        ok = keys[w] > 0.5
        for p in range(PAIRS):
            query, key = (packed[pair_at(part, w, p)] for part in range(2))
            for h, mask in enumerate(masks):
                scores = jnp.where(ok, dot_nt(key, query * mask), low)
                probs[w, 2 * p + h] = softmax(scores, 0).astype(BF)


def back_kernel(num, local, north, south, pad, cells, packed, probs, weight, *rest):
    blocks, rest = rest[:BLOCKS], rest[BLOCKS:]
    own, to_north, to_south, cot, kept, raw, wo, qkv, held, upstream, keys, grads, csem, ksem, osem, psem = rest
    cots = window_copies(1, local, north, south, cot, csem)
    loads = weight_copies(weight, kept, ksem)
    outs = block_copies(blocks, raw, osem)
    halves = [pltpu.make_async_copy(probs.at[w], held.at[w], psem.at[w]) for w in range(2)]
    halves.append(pltpu.make_async_copy(packed, qkv, psem.at[2]))
    start_all(outs + cots + halves)
    allowed_keys(num, pad, cells, keys)
    masks = head_masks()
    first = lax.broadcasted_iota(jnp.int32, (1, PAIR), 1) < HEAD
    wait_all(outs + cots)
    start_all(loads)
    in_order(raw, wo)
    for g in range(GROUPS):
        at = slice(g * GROUP, (g + 1) * GROUP)
        upstream[:, at] = dot_nt(cot[...], wo[at, :]).astype(BF)
    wait_all(halves)
    for w in range(2):
        ok = keys[w] > 0.5
        for p in range(PAIRS):
            query, key, value = (qkv[pair_at(part, w, p)] for part in range(3))
            above = upstream[pair_at(0, w, p)]
            dq, dk, dv = [], [], []
            for h, mask in enumerate(masks):
                given = held[w, 2 * p + h]
                wide = given.astype(F32)
                g_probs = dot_nt(value, above * mask)
                inner = jnp.sum(wide * g_probs, axis=0, keepdims=True)
                g_scores = jnp.where(ok, wide * (g_probs - inner), 0.0).astype(BF)
                dq.append(dot_tn(g_scores, key))
                dk.append(dot(g_scores, query))
                dv.append(dot(given, above))
            for part, (pair, scale) in enumerate(((dq, HEAD**-0.5), (dk, 1.0), (dv, 1.0))):
                grads[pair_at(part, w, p)] = (jnp.where(first, pair[0], pair[1]) * scale).astype(BF)
    wait_all(loads)
    for n in range(0, own.shape[1], GROUP):
        out = dot_nt(grads[...], kept[n : n + GROUP, :]).astype(BF)
        to_north[:, n : n + GROUP] = out[:PAD]
        own[:, n : n + GROUP] = out[PAD : PAD + WIN]
        to_south[:, n : n + GROUP] = out[PAD + WIN :]


def half_in_order(place, north_part, south_part):
    return dot_tn(place, jnp.concatenate([north_part, south_part], axis=0))


def project_kernel(num, own, from_south, from_north, sec, mir, table, *rest):
    blocks, (out, raw, wo, sems) = rest[:BLOCKS], rest[BLOCKS:]
    outs = block_copies(blocks, raw, sems)
    start_all(outs)
    place = one_hot(table, num[0])
    top = half_in_order(place, own[:PAD], from_north[...]).astype(BF)
    low = half_in_order(place, from_south[...], own[PAD:]).astype(BF)
    mixed = jnp.concatenate([top, low], axis=0)
    decoder = is_decoder()
    wait_all(outs)
    in_order(raw, wo)
    for n in range(0, out.shape[2], GROUP):
        at = slice(n, n + GROUP)
        both = sec[:, :, at].reshape(2 * HALF, GROUP).astype(F32)
        both += decoder * mir[:, :, at].reshape(2 * HALF, GROUP).astype(F32)
        out[:, :, at] = (both + dot(mixed, wo[:, at])).astype(BF).reshape(-1, LEV, GROUP)


def norm_back_kernel(num, own, from_south, from_north, sav, grd, mir, gain, table, out):
    half = pl.program_id(0)
    place = one_hot(table, num[0])
    north_part = jnp.where(half == 0, own[...], from_south[...])
    south_part = jnp.where(half == 0, from_north[...], own[...])
    grad = half_in_order(place, north_part, south_part) * gain[...]
    centered, scale = norm_parts(tokens(sav).astype(F32))
    hat = centered * scale
    inner = jnp.mean(grad * hat, axis=-1, keepdims=True)
    through = scale * (grad - jnp.mean(grad, axis=-1, keepdims=True) - hat * inner)
    cot = (tokens(grd).astype(F32) + (1.0 - is_decoder()) * tokens(mir).astype(F32)).astype(BF)
    out[...] = (cot.astype(F32) + through).astype(BF).reshape(out.shape)


def shift(value, axis, by):
    peers = lax.axis_size(axis)
    return lax.ppermute(value, axis, [(i, (i + by) % peers) for i in range(peers)])


def mirrored(value, sources):
    peers = lax.axis_size("section")
    return lax.ppermute(value, "section", [(i, peers - 1 - i) for i in sources])


def along_x(value, by):
    peers = lax.axis_size("sp")
    return lax.ppermute(
        value, "sp", [(i, i // X_SIZE * X_SIZE + (i + by) % X_SIZE) for i in range(peers)]
    )


def along_z(value, by):
    return shift(value, "sp", by * X_SIZE)


def whole():
    return pl.BlockSpec(memory_space=pltpu.VMEM)


def call(kernel, out_shape, micros, **kw):
    return pl.pallas_call(
        kernel,
        out_shape=out_shape,
        compiler_params=pltpu.CompilerParams(vmem_limit_bytes=VMEM),
        cost_estimate=pl.CostEstimate(flops=int(micros * 10**9), bytes_accessed=2**20, transcendentals=0),
        **kw,
    )


def shards(
    section_input,
    mirror_input,
    saved_input,
    output_grad,
    qkv_weight,
    out_weight,
    norm_gain,
    land_bias,
    shift_offset,
    land_sea,
    pole_pad,
):
    sections = lax.axis_size("section")
    width = section_input.shape[-1]
    smem = pl.BlockSpec(memory_space=pltpu.SMEM)
    any_ = pl.BlockSpec(memory_space=pl.ANY)
    places, cells, spots = map(jnp.asarray, (place_table(), cell_table(), land_table()))

    def flat(value):
        return value[0].transpose(0, 2, 1, 3).reshape(LATW * LON, LEV, width)

    sec, mir, sav, grd = map(flat, (section_input, mirror_input, saved_input, output_grad))

    def like(*shape):
        return jax.ShapeDtypeStruct(shape, BF)

    def fixed(*shape):
        return pl.BlockSpec(shape, lambda i: (0,) * len(shape))

    half = pl.BlockSpec((LATW * LON // 2, LEV, width), lambda i: (i, 0, 0))

    def prepared(kernel, arrays, count, name):
        return call(
            kernel,
            (like(count, WIN, width), like(count, PAD, width), like(count, PAD, width)),
            4.0,
            grid=(2,),
            in_specs=[smem]
            + [half] * len(arrays)
            + [fixed(1, width)] * 2
            + [fixed(LATW, LON), fixed(*places.shape), fixed(*spots.shape)],
            out_specs=(
                pl.BlockSpec((count, PAD, width), lambda i: (0, i, 0)),
                fixed(count, PAD, width),
                fixed(count, PAD, width),
            ),
            name=name,
        )(shift_offset, *arrays, norm_gain, land_bias, land_sea, places, spots)

    shard = out_weight[0]
    near = [along_x(shard, by) for by in (-1, 2, 1)]
    local, down, up = prepared(prepare_kernel, (sec, mir), 1, "prepare")
    near, down, up = lax.optimization_barrier((near, down, up))
    line = jnp.concatenate([shard, *near], axis=0)
    north = shift(down, "sp", 1)
    south = shift(up, "sp", -1)
    ups, downs = [along_z(line, 1)], [along_z(line, -1)]
    sav, line = lax.optimization_barrier((sav, line))
    local_back, down, up = prepared(prepare_back_kernel, (sav, grd, mir), 2, "prepare_back")
    north_back = shift(down, "sp", 1)
    south_back = shift(up, "sp", -1)
    ups.append(along_z(ups[-1], 1))
    downs.append(along_z(downs[-1], -1))
    weight = qkv_weight[0]
    inner = HEADS * HEAD
    dma = pltpu.SemaphoreType.DMA

    own, to_north, to_south = call(
        attend_kernel,
        (like(WIN, inner), like(PAD, inner), like(PAD, inner)),
        6.0,
        in_specs=[smem, any_, any_, any_, whole(), whole(), any_],
        out_specs=(whole(),) * 3,
        scratch_shapes=[
            pltpu.VMEM((2 * WIN, width), BF),
            pltpu.VMEM((width, 3 * inner), BF),
            pltpu.VMEM((2 * WIN, 3 * inner), BF),
            pltpu.VMEM((2, WIN, WIN), F32),
            dma((3,)),
            dma((LOADS,)),
        ],
        name="attend",
    )(shift_offset, local, north, south, pole_pad, cells, weight)
    from_south = shift(to_north, "sp", -1)
    from_north = shift(to_south, "sp", 1)
    above, below, own = lax.optimization_barrier((ups[-1], downs[-1], own))
    ups.append(along_z(above, 1))
    downs.append(along_z(below, -1))
    local_back, own = lax.optimization_barrier((local_back, own))
    packed, probs = call(
        probs_kernel,
        (like(2 * WIN, 3 * inner), like(2, HEADS, WIN, WIN)),
        6.0,
        in_specs=[smem, any_, any_, any_, whole(), whole(), any_],
        out_specs=(whole(),) * 2,
        scratch_shapes=[
            pltpu.VMEM((2 * WIN, width), BF),
            pltpu.VMEM((width, 3 * inner), BF),
            pltpu.VMEM((2, WIN, WIN), F32),
            dma((3,)),
            dma((LOADS,)),
        ],
        name="probs",
    )(shift_offset, local_back, north_back, south_back, pole_pad, cells, weight)
    above, below, probs = lax.optimization_barrier((ups[-1], downs[-1], probs))
    cut = width // 2
    ends = [along_z(above[:, :cut], 1), along_z(below[:, cut:], -1)]
    full = [line, *downs, *ends, *ups[::-1]]
    own_grad, grad_to_north, grad_to_south = call(
        back_kernel,
        (like(WIN, width), like(PAD, width), like(PAD, width)),
        15.0,
        in_specs=[smem, any_, any_, any_, whole(), whole()] + [any_] * (3 + BLOCKS),
        out_specs=(whole(),) * 3,
        scratch_shapes=[
            pltpu.VMEM((2 * WIN, width), BF),
            pltpu.VMEM((width, 3 * inner), BF),
            pltpu.VMEM((inner, width), BF),
            pltpu.VMEM((inner, width), BF),
            pltpu.VMEM((2 * WIN, 3 * inner), BF),
            pltpu.VMEM((2, HEADS, WIN, WIN), BF),
            pltpu.VMEM((2 * WIN, inner), BF),
            pltpu.VMEM((2, WIN, WIN), F32),
            pltpu.VMEM((2 * WIN, 3 * inner), BF),
            dma((3,)),
            dma((LOADS,)),
            dma((BLOCKS,)),
            dma((3,)),
        ],
        name="attend_back",
    )(shift_offset, local_back, north_back, south_back, pole_pad, cells, packed, probs, weight, *full)
    grad_from_south = shift(grad_to_north, "sp", -1)
    grad_from_north = shift(grad_to_south, "sp", 1)
    own, from_south, from_north, _ = lax.optimization_barrier((own, from_south, from_north, own_grad))
    block_out = call(
        project_kernel,
        like(LATW * LON, LEV, width),
        4.0,
        in_specs=[smem] + [whole()] * 6 + [any_] * BLOCKS,
        out_specs=whole(),
        scratch_shapes=[pltpu.VMEM((inner, width), BF), pltpu.VMEM((inner, width), BF), dma((BLOCKS,))],
        name="project",
    )(shift_offset, own, from_south, from_north, sec, mir, places, *full)
    grad_input = call(
        norm_back_kernel,
        like(LATW * LON, LEV, width),
        4.0,
        grid=(2,),
        in_specs=[smem, pl.BlockSpec((PAD, width), lambda i: (i, 0))]
        + [fixed(PAD, width)] * 2
        + [half] * 3
        + [fixed(1, width), fixed(*places.shape)],
        out_specs=half,
        name="norm_back",
    )(shift_offset, own_grad, grad_from_south, grad_from_north, sav, grd, mir, norm_gain, places)

    half_way = sections // 2
    block_out, grad_input = lax.optimization_barrier((block_out, grad_input))
    forward = shift(block_out, "section", 1)
    skips = mirrored(block_out, range(half_way - 1))
    backward = shift(grad_input, "section", -1)
    skip_grads = mirrored(grad_input, range(half_way + 1, sections))
    section = lax.axis_index("section")
    mirror_out = jnp.where(
        section >= half_way,
        jnp.where(section == half_way, forward, skips),
        jnp.where(section == half_way - 1, backward, skip_grads),
    )

    def back(value):
        return value.reshape(LATW, LON, LEV, width).transpose(0, 2, 1, 3)[None]

    return back(forward), back(backward), back(mirror_out)


def solution(mesh):
    return jax.shard_map(
        shards,
        mesh=mesh,
        in_specs=(
            P("section", "sp", None, None, None),
            P("section", "sp", None, None, None),
            P("section", "sp", None, None, None),
            P("section", "sp", None, None, None),
            P("section", None, None),
            P("section", "sp", None),
            P("section", None),
            P("section", None),
            P("section"),
            P("sp", None),
            P(),
        ),
        out_specs=(
            P("section", "sp", None, None, None),
            P("section", "sp", None, None, None),
            P("section", "sp", None, None, None),
        ),
        check_vma=False,
    )
```

```python
import functools

import jax
import jax.numpy as jnp
import numpy as np
from jax import lax
from jax.experimental import pallas as pl
from jax.experimental.pallas import tpu as pltpu
from jax.sharding import PartitionSpec as P

HEADS = 12
HEAD = 64
LATW = 12
LONW = 6
LEV = 2
LON = 12
HALF = LATW // 2 * LEV * LON
PART = HALF // 2
PAD = 80
WIN = 2 * PAD
PAIR = 2 * HEAD
PAIRS = HEADS // 2
GROUP = 2 * PAIR
X_SIZE = 4
BLOCKS = 9
LOADS = 12
GROUPS = HEADS * HEAD // GROUP
BF = jnp.bfloat16
F32 = jnp.float32
VMEM = 60 * 2**20


def row_parts():
    rows = np.arange(WIN)
    side, within = rows // PAD, rows % PAD
    spot = side * LONW + within % (LONW * LEV) // LEV
    return within < PART, within // (LONW * LEV), spot, within % LEV


def place_table():
    real, lat, spot, level = (part[:, None] for part in row_parts())
    token = np.arange(HALF)[None, :]
    same = real & (lat == token // (LON * LEV)) & (level == token % LEV)
    return np.where(same, (token // LEV % LON - spot) % LON, -1).astype(np.int32)


def cell_table():
    real, lat, spot, _ = (part[:, None] for part in row_parts())
    shifts = np.where(real, (np.arange(LON)[None, :] - spot) % LON, -1)
    return np.concatenate([shifts, lat], axis=1).astype(np.int32)


def land_table():
    token = np.arange(HALF)[:, None]
    return np.concatenate([token // (LON * LEV), token // LEV % LON], axis=1).astype(np.int32)


def dot(a, b):
    return jnp.dot(a, b, preferred_element_type=F32)


def dot_nt(a, b):
    return lax.dot_general(a, b, (((1,), (1,)), ((), ())), preferred_element_type=F32)


def dot_tn(a, b):
    return lax.dot_general(a, b, (((0,), (0,)), ((), ())), preferred_element_type=F32)


def one_hot(table_ref, offset):
    return (table_ref[...] == offset).astype(F32).astype(BF)


def is_decoder():
    return (lax.axis_index("section") >= lax.axis_size("section") // 2).astype(F32)


def tokens(ref):
    return ref[...].reshape(-1, ref.shape[-1])


def norm_parts(rows):
    centered = rows - jnp.mean(rows, axis=-1, keepdims=True)
    spread = jnp.mean(centered * centered, axis=-1, keepdims=True)
    return centered, lax.rsqrt(spread + 1e-05)


def spread(half, place, arrays, local, down, up):
    for i, rows in enumerate(arrays):
        placed = dot(place, rows).astype(BF)

        @pl.when(half == 0)
        def _():
            local[i] = placed[:PAD]
            up[i] = placed[PAD:]

        @pl.when(half == 1)
        def _():
            local[i] = placed[PAD:]
            down[i] = placed[:PAD]


def normed(rows, gain, bias, land, where):
    half = pl.program_id(0)
    lat, lon = where[:, 0:1], where[:, 1:2]
    cells = land[...].astype(F32)
    line = jnp.zeros((HALF, LON), F32)
    for row in range(LATW // 2):
        both = jnp.where(half == 0, cells[row : row + 1], cells[row + LATW // 2 : row + LATW // 2 + 1])
        line = jnp.where(lat == row, both, line)
    spots = lax.broadcasted_iota(jnp.int32, (HALF, LON), 1) == lon
    on_land = jnp.sum(jnp.where(spots, line, 0.0), axis=-1, keepdims=True)
    centered, scale = norm_parts(rows)
    return (centered * scale * gain[...] + on_land * bias[...]).astype(BF)


def prepare_kernel(num, sec, mir, gain, bias, land, table, where, local, down, up):
    start = tokens(sec).astype(F32) + is_decoder() * tokens(mir).astype(F32)
    rows = normed(start, gain, bias, land, where)
    spread(pl.program_id(0), one_hot(table, num[0]), [rows], local, down, up)


def prepare_back_kernel(num, sav, grd, mir, gain, bias, land, table, where, local, down, up):
    rows = normed(tokens(sav).astype(F32), gain, bias, land, where)
    cot = tokens(grd).astype(F32) + (1.0 - is_decoder()) * tokens(mir).astype(F32)
    spread(pl.program_id(0), one_hot(table, num[0]), [rows, cot.astype(BF)], local, down, up)


def valid_cells(pad, cells, offset, first_row):
    lat = cells[:, LON : LON + 1]
    line = jnp.zeros((WIN, LON), F32)
    for row in range(LATW // 2):
        line = jnp.where(lat == row, pad[pl.ds(first_row + row, 1), :].astype(F32), line)
    return jnp.max(jnp.where(cells[:, :LON] == offset, line, 0.0), axis=-1, keepdims=True)


def allowed_keys(num, pad, cells, keys):
    band, bands = lax.axis_index("sp"), lax.axis_size("sp")
    last = bands * LATW
    firsts = [lax.rem(band * LATW + last + by, last) for by in (-6, 0, 6, 12)]
    valid = [valid_cells(pad, cells, num[0], first) for first in firsts]
    row = lax.broadcasted_iota(jnp.int32, (WIN, WIN), 0)
    col = lax.broadcasted_iota(jnp.int32, (WIN, WIN), 1)
    apart = (row < PAD) != (col < PAD)
    for w, split in enumerate((band == 0, band == bands - 1)):
        at = slice(w * PAD, (w + 1) * PAD)
        real = jnp.concatenate([valid[2 * w][at], valid[2 * w + 1][at]], axis=0) > 0.5
        open_ = jnp.logical_not(apart & split)
        keys[w] = ((real & open_) | (row == col)).astype(F32)


def real_rows(axis):
    shape = (WIN, 1) if axis == 0 else (1, WIN)
    at = lax.broadcasted_iota(jnp.int32, shape, axis)
    return jnp.where(lax.rem(at, PAD) < PART, -1000000000.0, -3e38)


def head_masks():
    lane = lax.broadcasted_iota(jnp.int32, (1, PAIR), 1)
    return (lane < HEAD).astype(F32).astype(BF), (lane >= HEAD).astype(F32).astype(BF)


def softmax(scores, axis):
    expo = jnp.exp(scores - jnp.max(scores, axis=axis, keepdims=True))
    return expo * (1.0 / jnp.sum(expo, axis=axis, keepdims=True))


def window_copies(which, local, north, south, window, sems):
    pairs = (
        (north.at[which], window.at[pl.ds(0, PAD)]),
        (local.at[which], window.at[pl.ds(PAD, WIN)]),
        (south.at[which], window.at[pl.ds(PAD + WIN, PAD)]),
    )
    return [pltpu.make_async_copy(a, b, sems.at[i]) for i, (a, b) in enumerate(pairs)]


def weight_copies(weight, kept, sems):
    rows = weight.shape[0] // LOADS
    ats = [pl.ds(i * rows, rows) for i in range(LOADS)]
    return [pltpu.make_async_copy(weight.at[at], kept.at[at], sems.at[i]) for i, at in enumerate(ats)]


def start_all(copies):
    for copy in copies:
        copy.start()


def wait_all(copies):
    for copy in copies:
        copy.wait()


def columns(part, g):
    return slice((part * GROUPS + g) * GROUP, (part * GROUPS + g + 1) * GROUP)


def pack_all(window, kept, packed, loads):
    wait_all(loads)
    for g in range(GROUPS):
        for part in range(3):
            out = dot(window[...], kept[:, columns(part, g)])
            packed[:, columns(part, g)] = (out * HEAD**-0.5 if part == 0 else out).astype(BF)


def pair_at(part, w, p):
    start = part * HEADS * HEAD + p * PAIR
    return slice(w * WIN, (w + 1) * WIN), slice(start, start + PAIR)


def attend_kernel(
    num, local, north, south, pad, cells, weight, own, to_north, to_south,
    window, kept, packed, keys, wsem, ksem,
):
    moves = window_copies(0, local, north, south, window, wsem)
    loads = weight_copies(weight, kept, ksem)
    start_all(moves + loads)
    allowed_keys(num, pad, cells, keys)
    masks = head_masks()
    first = lax.broadcasted_iota(jnp.int32, (1, PAIR), 1) < HEAD
    low = real_rows(1)
    wait_all(moves)
    pack_all(window, kept, packed, loads)
    for w in range(2):
        ok = keys[w].T > 0.5
        for p in range(PAIRS):
            query, key, value = (packed[pair_at(part, w, p)] for part in range(3))
            mixed = []
            for mask in masks:
                scores = jnp.where(ok, dot_nt(query * mask, key), low)
                mixed.append(dot(softmax(scores, -1).astype(BF), value))
            out = jnp.where(first, mixed[0], mixed[1]).astype(BF)
            to = slice(p * PAIR, (p + 1) * PAIR)
            if w == 0:
                to_north[:, to] = out[:PAD]
                own[:PAD, to] = out[PAD:]
            else:
                own[PAD:, to] = out[:PAD]
                to_south[:, to] = out[PAD:]


def block_copies(blocks, raw, sems):
    planes = lax.axis_size("sp") // X_SIZE
    rows, width = raw.shape[0] // planes, raw.shape[1]
    plane = lax.div(lax.axis_index("sp"), X_SIZE)
    out = []
    for i, block in enumerate(blocks):
        j = min(i, planes // 2) if i <= planes // 2 + 1 else i - 1
        at = pl.ds(pl.multiple_of(lax.rem(plane + j, planes) * rows, rows), rows)
        to = raw.at[at] if block.shape[1] == width else raw.at[at, pl.ds((i - planes // 2) * width // 2, width // 2)]
        out.append(pltpu.make_async_copy(block, to, sems.at[i]))
    return out


def in_order(raw, wo):
    planes = lax.axis_size("sp") // X_SIZE
    rows = raw.shape[0] // planes
    turn = lax.rem(lax.axis_index("sp"), X_SIZE) * (rows // X_SIZE)
    row = lax.broadcasted_iota(jnp.int32, (rows, rows), 0)
    col = lax.broadcasted_iota(jnp.int32, (rows, rows), 1)
    place = (row == lax.rem(col + turn, rows)).astype(F32).astype(BF)
    for j in range(planes):
        at = slice(j * rows, (j + 1) * rows)
        wo[at] = dot(place, raw[at]).astype(BF)


def probs_kernel(
    num, local, north, south, pad, cells, weight, packed_out, probs_out,
    window, kept, keys, packed, probs, wsem, ksem, osem,
):
    moves = window_copies(0, local, north, south, window, wsem)
    loads = weight_copies(weight, kept, ksem)
    start_all(moves + loads)
    allowed_keys(num, pad, cells, keys)
    masks = head_masks()
    low = real_rows(0)
    wait_all(moves)
    pack_all(window, kept, packed, loads)
    stores = [pltpu.make_async_copy(packed, packed_out, osem.at[2])]
    stores += [pltpu.make_async_copy(probs.at[w], probs_out.at[w], osem.at[w]) for w in range(2)]
    stores[0].start()
    for w in range(2):
        ok = keys[w] > 0.5
        for p in range(PAIRS):
            query, key = (packed[pair_at(part, w, p)] for part in range(2))
            for h, mask in enumerate(masks):
                scores = jnp.where(ok, dot_nt(key, query * mask), low)
                probs[w, 2 * p + h] = softmax(scores, 0).astype(BF)
        stores[1 + w].start()
    wait_all(stores)


def back_kernel(num, local, north, south, pad, cells, packed, probs, weight, *rest):
    blocks, rest = rest[:BLOCKS], rest[BLOCKS:]
    own, to_north, to_south, cot, kept, raw, wo, qkv, held, upstream, keys, grads, csem, ksem, osem, psem = rest
    cots = window_copies(1, local, north, south, cot, csem)
    loads = weight_copies(weight, kept, ksem)
    outs = block_copies(blocks, raw, osem)
    halves = [pltpu.make_async_copy(probs.at[w], held.at[w], psem.at[w]) for w in range(2)]
    halves.append(pltpu.make_async_copy(packed, qkv, psem.at[2]))
    start_all(outs + cots + halves)
    allowed_keys(num, pad, cells, keys)
    masks = head_masks()
    first = lax.broadcasted_iota(jnp.int32, (1, PAIR), 1) < HEAD
    wait_all(outs + cots)
    start_all(loads)
    in_order(raw, wo)
    for g in range(GROUPS):
        at = slice(g * GROUP, (g + 1) * GROUP)
        upstream[:, at] = dot_nt(cot[...], wo[at, :]).astype(BF)
    wait_all(halves)
    for w in range(2):
        ok = keys[w] > 0.5
        for p in range(PAIRS):
            query, key, value = (qkv[pair_at(part, w, p)] for part in range(3))
            above = upstream[pair_at(0, w, p)]
            dq, dk, dv = [], [], []
            for h, mask in enumerate(masks):
                given = held[w, 2 * p + h]
                wide = given.astype(F32)
                g_probs = dot_nt(value, above * mask)
                inner = jnp.sum(wide * g_probs, axis=0, keepdims=True)
                g_scores = jnp.where(ok, wide * (g_probs - inner), 0.0).astype(BF)
                dq.append(dot_tn(g_scores, key))
                dk.append(dot(g_scores, query))
                dv.append(dot(given, above))
            for part, (pair, scale) in enumerate(((dq, HEAD**-0.5), (dk, 1.0), (dv, 1.0))):
                grads[pair_at(part, w, p)] = (jnp.where(first, pair[0], pair[1]) * scale).astype(BF)
    wait_all(loads)
    for n in range(0, own.shape[1], GROUP):
        out = dot_nt(grads[...], kept[n : n + GROUP, :]).astype(BF)
        to_north[:, n : n + GROUP] = out[:PAD]
        own[:, n : n + GROUP] = out[PAD : PAD + WIN]
        to_south[:, n : n + GROUP] = out[PAD + WIN :]


def half_in_order(place, north_part, south_part):
    return dot_tn(place, jnp.concatenate([north_part, south_part], axis=0))


def project_kernel(num, own, from_south, from_north, sec, mir, table, *rest):
    blocks, (out, raw, wo, sems) = rest[:BLOCKS], rest[BLOCKS:]
    outs = block_copies(blocks, raw, sems)
    start_all(outs)
    place = one_hot(table, num[0])
    top = half_in_order(place, own[:PAD], from_north[...]).astype(BF)
    low = half_in_order(place, from_south[...], own[PAD:]).astype(BF)
    mixed = jnp.concatenate([top, low], axis=0)
    decoder = is_decoder()
    wait_all(outs)
    in_order(raw, wo)
    for n in range(0, out.shape[2], GROUP):
        at = slice(n, n + GROUP)
        both = sec[:, :, at].reshape(2 * HALF, GROUP).astype(F32)
        both += decoder * mir[:, :, at].reshape(2 * HALF, GROUP).astype(F32)
        out[:, :, at] = (both + dot(mixed, wo[:, at])).astype(BF).reshape(-1, LEV, GROUP)


def norm_back_kernel(num, own, from_south, from_north, sav, grd, mir, gain, table, out):
    half = pl.program_id(0)
    place = one_hot(table, num[0])
    north_part = jnp.where(half == 0, own[...], from_south[...])
    south_part = jnp.where(half == 0, from_north[...], own[...])
    grad = half_in_order(place, north_part, south_part) * gain[...]
    centered, scale = norm_parts(tokens(sav).astype(F32))
    hat = centered * scale
    inner = jnp.mean(grad * hat, axis=-1, keepdims=True)
    through = scale * (grad - jnp.mean(grad, axis=-1, keepdims=True) - hat * inner)
    cot = (tokens(grd).astype(F32) + (1.0 - is_decoder()) * tokens(mir).astype(F32)).astype(BF)
    out[...] = (cot.astype(F32) + through).astype(BF).reshape(out.shape)


def shift(value, axis, by):
    peers = lax.axis_size(axis)
    return lax.ppermute(value, axis, [(i, (i + by) % peers) for i in range(peers)])


def mirrored(value, sources):
    peers = lax.axis_size("section")
    return lax.ppermute(value, "section", [(i, peers - 1 - i) for i in sources])


def along_x(value, by):
    peers = lax.axis_size("sp")
    return lax.ppermute(
        value, "sp", [(i, i // X_SIZE * X_SIZE + (i + by) % X_SIZE) for i in range(peers)]
    )


def along_z(value, by):
    return shift(value, "sp", by * X_SIZE)


def whole():
    return pl.BlockSpec(memory_space=pltpu.VMEM)


def call(kernel, out_shape, micros, **kw):
    return pl.pallas_call(
        kernel,
        out_shape=out_shape,
        compiler_params=pltpu.CompilerParams(vmem_limit_bytes=VMEM),
        cost_estimate=pl.CostEstimate(flops=int(micros * 10**9), bytes_accessed=2**20, transcendentals=0),
        **kw,
    )


def shards(
    section_input,
    mirror_input,
    saved_input,
    output_grad,
    qkv_weight,
    out_weight,
    norm_gain,
    land_bias,
    shift_offset,
    land_sea,
    pole_pad,
):
    sections = lax.axis_size("section")
    width = section_input.shape[-1]
    smem = pl.BlockSpec(memory_space=pltpu.SMEM)
    any_ = pl.BlockSpec(memory_space=pl.ANY)
    places, cells, spots = map(jnp.asarray, (place_table(), cell_table(), land_table()))

    def flat(value):
        return value[0].transpose(0, 2, 1, 3).reshape(LATW * LON, LEV, width)

    sec, mir, sav, grd = map(flat, (section_input, mirror_input, saved_input, output_grad))

    def like(*shape):
        return jax.ShapeDtypeStruct(shape, BF)

    def fixed(*shape):
        return pl.BlockSpec(shape, lambda i: (0,) * len(shape))

    half = pl.BlockSpec((LATW * LON // 2, LEV, width), lambda i: (i, 0, 0))

    def prepared(kernel, arrays, count, name):
        return call(
            kernel,
            (like(count, WIN, width), like(count, PAD, width), like(count, PAD, width)),
            4.0,
            grid=(2,),
            in_specs=[smem]
            + [half] * len(arrays)
            + [fixed(1, width)] * 2
            + [fixed(LATW, LON), fixed(*places.shape), fixed(*spots.shape)],
            out_specs=(
                pl.BlockSpec((count, PAD, width), lambda i: (0, i, 0)),
                fixed(count, PAD, width),
                fixed(count, PAD, width),
            ),
            name=name,
        )(shift_offset, *arrays, norm_gain, land_bias, land_sea, places, spots)

    shard = out_weight[0]
    near = [along_x(shard, by) for by in (-1, 2, 1)]
    local, down, up = prepared(prepare_kernel, (sec, mir), 1, "prepare")
    near, down, up = lax.optimization_barrier((near, down, up))
    line = jnp.concatenate([shard, *near], axis=0)
    north = shift(down, "sp", 1)
    south = shift(up, "sp", -1)
    ups, downs = [along_z(line, 1)], [along_z(line, -1)]
    sav, line = lax.optimization_barrier((sav, line))
    local_back, down, up = prepared(prepare_back_kernel, (sav, grd, mir), 2, "prepare_back")
    north_back = shift(down, "sp", 1)
    south_back = shift(up, "sp", -1)
    ups.append(along_z(ups[-1], 1))
    downs.append(along_z(downs[-1], -1))
    weight = qkv_weight[0]
    inner = HEADS * HEAD
    dma = pltpu.SemaphoreType.DMA

    own, to_north, to_south = call(
        attend_kernel,
        (like(WIN, inner), like(PAD, inner), like(PAD, inner)),
        6.0,
        in_specs=[smem, any_, any_, any_, whole(), whole(), any_],
        out_specs=(whole(),) * 3,
        scratch_shapes=[
            pltpu.VMEM((2 * WIN, width), BF),
            pltpu.VMEM((width, 3 * inner), BF),
            pltpu.VMEM((2 * WIN, 3 * inner), BF),
            pltpu.VMEM((2, WIN, WIN), F32),
            dma((3,)),
            dma((LOADS,)),
        ],
        name="attend",
    )(shift_offset, local, north, south, pole_pad, cells, weight)
    from_south = shift(to_north, "sp", -1)
    from_north = shift(to_south, "sp", 1)
    above, below, own = lax.optimization_barrier((ups[-1], downs[-1], own))
    ups.append(along_z(above, 1))
    downs.append(along_z(below, -1))
    local_back, own = lax.optimization_barrier((local_back, own))
    packed, probs = call(
        probs_kernel,
        (like(2 * WIN, 3 * inner), like(2, HEADS, WIN, WIN)),
        6.0,
        in_specs=[smem, any_, any_, any_, whole(), whole(), any_],
        out_specs=(any_,) * 2,
        scratch_shapes=[
            pltpu.VMEM((2 * WIN, width), BF),
            pltpu.VMEM((width, 3 * inner), BF),
            pltpu.VMEM((2, WIN, WIN), F32),
            pltpu.VMEM((2 * WIN, 3 * inner), BF),
            pltpu.VMEM((2, HEADS, WIN, WIN), BF),
            dma((3,)),
            dma((LOADS,)),
            dma((3,)),
        ],
        name="probs",
    )(shift_offset, local_back, north_back, south_back, pole_pad, cells, weight)
    above, below, probs = lax.optimization_barrier((ups[-1], downs[-1], probs))
    cut = width // 2
    ends = [along_z(above[:, :cut], 1), along_z(below[:, cut:], -1)]
    full = [line, *downs, *ends, *ups[::-1]]
    own_grad, grad_to_north, grad_to_south = call(
        back_kernel,
        (like(WIN, width), like(PAD, width), like(PAD, width)),
        15.0,
        in_specs=[smem, any_, any_, any_, whole(), whole()] + [any_] * (3 + BLOCKS),
        out_specs=(whole(),) * 3,
        scratch_shapes=[
            pltpu.VMEM((2 * WIN, width), BF),
            pltpu.VMEM((width, 3 * inner), BF),
            pltpu.VMEM((inner, width), BF),
            pltpu.VMEM((inner, width), BF),
            pltpu.VMEM((2 * WIN, 3 * inner), BF),
            pltpu.VMEM((2, HEADS, WIN, WIN), BF),
            pltpu.VMEM((2 * WIN, inner), BF),
            pltpu.VMEM((2, WIN, WIN), F32),
            pltpu.VMEM((2 * WIN, 3 * inner), BF),
            dma((3,)),
            dma((LOADS,)),
            dma((BLOCKS,)),
            dma((3,)),
        ],
        name="attend_back",
    )(shift_offset, local_back, north_back, south_back, pole_pad, cells, packed, probs, weight, *full)
    grad_from_south = shift(grad_to_north, "sp", -1)
    grad_from_north = shift(grad_to_south, "sp", 1)
    own, from_south, from_north, _ = lax.optimization_barrier((own, from_south, from_north, own_grad))
    block_out = call(
        project_kernel,
        like(LATW * LON, LEV, width),
        4.0,
        in_specs=[smem] + [whole()] * 6 + [any_] * BLOCKS,
        out_specs=whole(),
        scratch_shapes=[pltpu.VMEM((inner, width), BF), pltpu.VMEM((inner, width), BF), dma((BLOCKS,))],
        name="project",
    )(shift_offset, own, from_south, from_north, sec, mir, places, *full)
    grad_input = call(
        norm_back_kernel,
        like(LATW * LON, LEV, width),
        4.0,
        grid=(2,),
        in_specs=[smem, pl.BlockSpec((PAD, width), lambda i: (i, 0))]
        + [fixed(PAD, width)] * 2
        + [half] * 3
        + [fixed(1, width), fixed(*places.shape)],
        out_specs=half,
        name="norm_back",
    )(shift_offset, own_grad, grad_from_south, grad_from_north, sav, grd, mir, norm_gain, places)

    half_way = sections // 2
    forward = shift(block_out, "section", 1)
    skips = mirrored(block_out, range(half_way - 1))
    backward = shift(grad_input, "section", -1)
    skip_grads = mirrored(grad_input, range(half_way + 1, sections))
    section = lax.axis_index("section")
    mirror_out = jnp.where(
        section >= half_way,
        jnp.where(section == half_way, forward, skips),
        jnp.where(section == half_way - 1, backward, skip_grads),
    )

    def back(value):
        return value.reshape(LATW, LON, LEV, width).transpose(0, 2, 1, 3)[None]

    return back(forward), back(backward), back(mirror_out)


def solution(mesh):
    return jax.shard_map(
        shards,
        mesh=mesh,
        in_specs=(
            P("section", "sp", None, None, None),
            P("section", "sp", None, None, None),
            P("section", "sp", None, None, None),
            P("section", "sp", None, None, None),
            P("section", None, None),
            P("section", "sp", None),
            P("section", None),
            P("section", None),
            P("section"),
            P("sp", None),
            P(),
        ),
        out_specs=(
            P("section", "sp", None, None, None),
            P("section", "sp", None, None, None),
            P("section", "sp", None, None, None),
        ),
        check_vma=False,
    )
```
